32 devices in a mesh: groups: 2 (over x), store: 16 (over z, y, core).
Axes of the slice: x: 2, y: 2, z: 4, core: 2. Of those that a mesh axis runs over, the one named last changes fastest.
Arguments:
- sources: bfloat16 [16384, 512], P(('groups', 'store')), parts along dimension 0, may hold values from -1800 to 1800
- self_terms: float32 [2, 8192], P(None, 'store'), may hold values from 0.5 to 2
- near_tiles: bfloat16 [2, 32, 5, 256, 256], P(None, 'store'), may hold values from -1 to 1
- near_cols: int32 [32, 5], P('store'), may hold values from 0 to 31, as said below
- near_count: int32 [32], P('store'), may hold values from 1 to 5, as said below
- far_cols: int32 [32, 6], P('store'), may hold values from 0 to 31, as said below
- basis_left: bfloat16 [32, 256, 32], P('store'), may hold values from -2 to 2
- basis_right: bfloat16 [32, 256, 32], P('store'), may hold values from -2 to 2
- couplings: bfloat16 [2, 32, 6, 32, 32], P(None, 'store'), may hold values from -1 to 1
Outputs:
- images: float32 [2, 16384, 512], P(None, ('groups', 'store')), parts along dimension 1
- heights: float32 [4, 512], P('groups'), parts along dimension 0
- norms: float32 [4, 512], P('groups'), parts along dimension 0
The draws below stay inside these ranges and needn't reach their ends.
There are 2 independent parts, one for each index of `groups`. The reference program is written for one: setup_inputs(seed, part) draws one part's arguments, and reference() takes and returns one part's arrays. A program takes and returns all parts, laid end to end along the dimension named above; an argument that names none is the same for every part. Nothing has to cross between parts.
Inputs may be any that keep to these rules, and one draw needn't show every extreme that they name: `near_cols`: the slots of row block i name the blocks i - 2 to i + 2, cyclically, each once, in a drawn order. Slots 0 to near_count - 1 of a row block are live; block 0 has all 5. `far_cols`: a far-field block lies more than 2 blocks from its row block, cyclically.
All inputs are finite; a program needn't handle non-finite values.
Results may differ from the reference program's by a relative error of at most 0.011.
Values may be sent and summed in bfloat16 or wider, within the bound.
A program may use at most 128 MiB of HBM per device.

```python
import math
import jax
import jax.numpy as jnp
from jax import lax

BLOCK = 256
SOURCES = 512
RANK = 32
REACH = 2
FAR = 6
NEAR = 5
BLOCKS = 32
PANELS = 8192


def draw_sources(key, part):
    key_rows = jax.random.fold_in(key, 0)
    key_cols = jax.random.fold_in(key, 1)
    key_base = jax.random.fold_in(key, 2)
    key_level = jax.random.fold_in(key, 4)
    key_sign = jax.random.fold_in(key, 5)
    key_block = jax.random.fold_in(key, 6)
    position = jnp.arange(PANELS, dtype=jnp.float32) / PANELS
    row_scale = jnp.exp(position * math.log(3.0)) * jnp.exp(jax.random.uniform(key_rows, (PANELS,)) * math.log(10.0))
    col_scale = jnp.exp(jax.random.uniform(key_cols, (SOURCES,)) * math.log(10.0))
    level = 0.7 + 0.6 * jax.random.uniform(key_level, (SOURCES,))
    signs = jnp.where(jax.random.bernoulli(key_sign, 0.5, (SOURCES,)), 1.0, -1.0)
    shared = (signs * level)[None, :]
    block_part = 0.5 * jax.random.normal(key_block, (BLOCKS, 1, SOURCES))
    block_part = jnp.broadcast_to(block_part, (BLOCKS, BLOCK, SOURCES)).reshape(PANELS, SOURCES)
    noise = jax.random.normal(key_base, (PANELS, SOURCES))
    draws_base = 0.6 * noise + shared + block_part
    values = jnp.clip(draws_base, -6.0, 6.0) * row_scale[:, None] * col_scale[None, :]
    return values.astype(jnp.bfloat16)


def draw_near_tiles(key, part):
    key_noise, key_level = jax.random.split(jax.random.fold_in(key, 21), 2)
    spread = 1.0 / math.sqrt(NEAR * BLOCK)
    level = 0.5 / BLOCK * (0.5 + jax.random.uniform(key_level, (2, BLOCKS, NEAR, 1, 1)))
    noise = jnp.clip(jax.random.normal(key_noise, (2, BLOCKS, NEAR, BLOCK, BLOCK)), -4.0, 4.0)
    return (level + spread * noise).astype(jnp.bfloat16)


def basis_draw(key, width):
    key_noise, key_mono = jax.random.split(key, 2)
    spread = 1.0 / math.sqrt(width)
    noise = jnp.clip(jax.random.normal(key_noise, (BLOCKS, BLOCK, RANK)), -4.0, 4.0) * spread
    mono = spread * (0.75 + 0.5 * jax.random.uniform(key_mono, (BLOCKS, BLOCK, RANK)))
    first_col = (jnp.arange(RANK, dtype=jnp.int32) == 0)[None, None, :]
    return jnp.where(first_col, mono, noise).astype(jnp.bfloat16)


def draw_basis_left(key, part):
    return basis_draw(jax.random.fold_in(key, 31), RANK)


def draw_basis_right(key, part):
    return basis_draw(jax.random.fold_in(key, 41), BLOCK)


def draw_couplings(key, part):
    key_noise, key_mono = jax.random.split(jax.random.fold_in(key, 51), 2)
    spread = 1.0 / math.sqrt(FAR * RANK)
    shape_all = (2, BLOCKS, FAR, RANK, RANK)
    noise = jnp.clip(jax.random.normal(key_noise, shape_all), -4.0, 4.0) * spread
    rows_at = jnp.arange(RANK, dtype=jnp.int32)[:, None]
    cols_at = jnp.arange(RANK, dtype=jnp.int32)[None, :]
    column_zero = cols_at == 0
    noise = jnp.where(column_zero, noise / math.sqrt(BLOCK), noise)
    mono_level = 0.6 * math.sqrt(RANK) / (FAR * math.sqrt(BLOCK))
    mono = mono_level * (0.5 + jax.random.uniform(key_mono, shape_all))
    corner = (rows_at == 0) & column_zero
    return jnp.where(corner, mono, noise).astype(jnp.bfloat16)


def draw_near_cols(key, part):
    scores = jax.random.randint(key, (BLOCKS, NEAR), 0, 1 << 20) * NEAR + jnp.arange(NEAR, dtype=jnp.int32)[None, :]
    orders = jnp.argsort(scores, axis=1).astype(jnp.int32)
    rows_at = jnp.arange(BLOCKS, dtype=jnp.int32)[:, None]
    return ((rows_at + orders - REACH) % BLOCKS).astype(jnp.int32)


def draw_near_count(key, part):
    key_first, key_second = jax.random.split(jax.random.fold_in(key, 7), 2)
    first_draw = jax.random.randint(key_first, (BLOCKS,), 1, NEAR + 1)
    second_draw = jax.random.randint(key_second, (BLOCKS,), 1, NEAR + 1)
    counts = jnp.minimum(first_draw, second_draw).at[0].set(NEAR)
    return counts.astype(jnp.int32)


def draw_far_cols(key, part):
    offsets = jax.random.randint(jax.random.fold_in(key, 11), (BLOCKS, FAR), REACH + 1, BLOCKS - REACH)
    rows_at = jnp.arange(BLOCKS, dtype=jnp.int32)[:, None]
    return ((rows_at + offsets) % BLOCKS).astype(jnp.int32)


def level_of(key, dims, shards, low, high):
    loudness = 1.0
    for axis_at, parts in shards:
        draws = jax.random.uniform(jax.random.fold_in(jax.random.fold_in(key, 6), axis_at), (parts,), jnp.float32, low / len(shards), high / len(shards))
        loudness = loudness * jnp.repeat(jnp.exp(draws), dims[axis_at] // parts).reshape((-1,) + (1,) * (len(dims) - 1 - axis_at))
    return loudness


def setup_inputs(seed: int = 0, part: int = 0) -> dict:
    streams_of = jax.random.split(jax.random.key(seed), 10)
    part_splits = jax.random.split(jax.random.fold_in(streams_of[9], part), 10)
    sources = draw_sources(jax.random.fold_in(jax.random.fold_in(streams_of[9], part), 71), part)
    self_terms = jnp.clip(jnp.exp(math.log(2.0) - 1.3862944 * jax.random.uniform(streams_of[1], (2, PANELS), jnp.float32) ** level_of(streams_of[1], (2, PANELS), ((1, 16),), -0.2, 0.2)), 0.5, 2.0)
    near_tiles = draw_near_tiles(jax.random.fold_in(streams_of[9], 71), part)
    near_cols = draw_near_cols(jax.random.fold_in(streams_of[9], 71), part)
    near_count = draw_near_count(jax.random.fold_in(streams_of[9], 71), part)
    far_cols = draw_far_cols(jax.random.fold_in(streams_of[9], 71), part)
    basis_left = draw_basis_left(jax.random.fold_in(streams_of[9], 71), part)
    basis_right = draw_basis_right(jax.random.fold_in(streams_of[9], 71), part)
    couplings = draw_couplings(jax.random.fold_in(streams_of[9], 71), part)
    return {"sources": sources, "self_terms": self_terms, "near_tiles": near_tiles, "near_cols": near_cols, "near_count": near_count, "far_cols": far_cols, "basis_left": basis_left, "basis_right": basis_right, "couplings": couplings}


EPSILON = 1e-06

def apply_operator(inputs, self_terms, near_tiles, near_cols, near_count, far_cols, basis_left, basis_right, couplings):
    coeffs = jnp.einsum('bpr,kbps->kbrs', basis_right.astype(jnp.float32), inputs.astype(jnp.float32)).astype(jnp.bfloat16)
    slot_ids = jnp.arange(NEAR, dtype=jnp.int32)

    def one_block(row_id):
        tiles_row = near_tiles[:, row_id].astype(jnp.float32)
        taken = inputs[:, near_cols[row_id]].astype(jnp.float32)
        weight = (slot_ids < near_count[row_id]).astype(jnp.float32)
        taken = taken * weight[None, :, None, None]
        taken = jnp.broadcast_to(taken, (2,) + taken.shape[1:])
        near_part = jnp.einsum('okpq,okqs->ops', tiles_row, taken)
        picked = coeffs[:, far_cols[row_id]].astype(jnp.float32)
        picked = jnp.broadcast_to(picked, (2,) + picked.shape[1:])
        reduced = jnp.einsum('ofrq,ofqs->ors', couplings[:, row_id].astype(jnp.float32), picked).astype(jnp.bfloat16)
        far_part = jnp.einsum('pr,ors->ops', basis_left[row_id].astype(jnp.float32), reduced.astype(jnp.float32)).astype(jnp.bfloat16)
        return near_part + far_part.astype(jnp.float32)
    rows_out = lax.map(one_block, jnp.arange(BLOCKS, dtype=jnp.int32))
    diagonal = self_terms.reshape(2, BLOCKS, BLOCK)
    return jnp.transpose(rows_out, (1, 0, 2, 3)) + diagonal[..., None] * inputs.astype(jnp.float32)

def reference(sources, self_terms, near_tiles, near_cols, near_count, far_cols, basis_left, basis_right, couplings):
    operands = (self_terms, near_tiles, near_cols, near_count, far_cols, basis_left, basis_right, couplings)
    source_f = sources.astype(jnp.float32).reshape(BLOCKS, BLOCK, SOURCES)
    scale_sq = lax.optimization_barrier(jnp.sum(source_f * source_f, axis=(0, 1))) / PANELS
    first_vec = (source_f / jnp.sqrt(scale_sq + EPSILON)).astype(jnp.bfloat16)
    image_one = apply_operator(first_vec[None], *operands)
    first_f = first_vec.astype(jnp.float32)
    heights = lax.optimization_barrier(jnp.sum(first_f[None] * image_one, axis=(1, 2))) / PANELS
    remain = image_one - heights[:, None, None, :] * first_f[None]
    norms = jnp.sqrt(lax.optimization_barrier(jnp.sum(remain * remain, axis=(1, 2))) / PANELS + EPSILON)
    second_vec = (remain / norms[:, None, None, :]).astype(jnp.bfloat16)
    image_two = apply_operator(second_vec, *operands)
    return (image_two.reshape(2, PANELS, SOURCES), heights, norms)
```

```python
import functools

import jax
import jax.numpy as jnp
from jax import lax
from jax.experimental import pallas as pl
from jax.experimental.pallas import tpu as pltpu
from jax.sharding import PartitionSpec as P

REACH = 2
EPSILON = 1e-06
CHUNK = 128
GROUP = 16
RELAY1 = (False, True)
CORES = 2
TINY = 1e-30
MESH = pl.DeviceIdType.MESH
F32 = jnp.float32
BF16 = jnp.bfloat16


def grid_of(devices):
    chips = devices // CORES
    inner = 1
    while inner * inner * 4 <= chips:
        inner *= 2
    return chips // inner, inner


def split3(x):
    high = x.astype(BF16)
    rest = x - high.astype(F32)
    mid = rest.astype(BF16)
    low = (rest - mid.astype(F32)).astype(BF16)
    return [high.astype(F32), mid.astype(F32), low.astype(F32)]


def kernel(
    devices,
    cols_ref,
    count_ref,
    far_ref,
    src_hbm,
    self_hbm,
    tiles_hbm,
    left_hbm,
    right_hbm,
    coup_hbm,
    out_any,
    heights_any,
    norms_any,
    self_ref,
    tiles_ref,
    left_ref,
    right_ref,
    coup_ref,
    out_ref,
    heights_ref,
    norms_ref,
    w_ref,
    g_ref,
    self_col,
    u1,
    u2,
    uw,
    z1,
    z2,
    zsel,
    y_ref,
    in_sem,
    src_sem,
    out_sem,
    h1_send,
    h1_recv,
    h2_send,
    h2_recv,
    y_send,
    y_recv,
    r_send,
    r_recv,
    q_send,
    f_send,
    f_recv,
):
    me = lax.axis_index("store")
    planes, inner = grid_of(devices)
    chips = devices // CORES
    chip = me // CORES
    core = me % CORES
    plane = chip // inner
    place = chip % inner
    half = planes // 2
    partner = chip * CORES + (1 - core)
    right = (me + 1) % devices
    left = (me + devices - 1) % devices
    local, near, size = tiles_ref.shape[1:4]
    far, rank = coup_ref.shape[2:4]
    rows = local * size
    width = u1.shape[2]
    chunks = u1.shape[0]
    blocks = devices * local
    panels = blocks * size
    pieces = rank // GROUP

    def device_at(a, b, k):
        return (a * inner + b) * CORES + k

    def remote(src, dst, send, recv, peer):
        return pltpu.make_async_remote_copy(
            src_ref=src,
            dst_ref=dst,
            send_sem=send,
            recv_sem=recv,
            device_id={"store": peer},
            device_id_type=MESH,
        )

    barrier = pltpu.get_barrier_semaphore()

    def greet(peer):
        pl.semaphore_signal(barrier, inc=1, device_id={"store": peer}, device_id_type=MESH)

    greet(left)
    greet(right)
    for t in range(1, inner):
        greet(device_at(plane, (place + t) % inner, core))
    for t in range(1, planes):
        greet(device_at((plane + t) % planes, place, core))

    def own_copy(c):
        return pltpu.make_async_copy(
            src_hbm.at[:, pl.ds(c * width, width)],
            u1.at[c, pl.ds(rows, rows)],
            src_sem.at[c],
        )

    loads = [
        pltpu.make_async_copy(hbm, vmem, in_sem.at[i])
        for i, (hbm, vmem) in enumerate(
            (
                (right_hbm, right_ref),
                (tiles_hbm, tiles_ref),
                (left_hbm, left_ref),
                (coup_hbm, coup_ref),
                (self_hbm, self_ref),
            )
        )
    ]
    loads[0].start()
    for c in range(chunks):
        own_copy(c).start()
    for load in loads[1:]:
        load.start()

    pl.semaphore_wait(barrier, 2 + inner - 1 + planes - 1)

    def halo1(c):
        own = src_hbm.at[:, pl.ds(c * width, width)]
        return (
            remote(own, u1.at[c, pl.ds(0, rows)], h1_send.at[c, 0], h1_recv.at[c, 0], right),
            remote(own, u1.at[c, pl.ds(2 * rows, rows)], h1_send.at[c, 1], h1_recv.at[c, 1], left),
        )

    def halo2(c, o):
        field = u2.at[c, o]
        own = field.at[pl.ds(rows, rows)]
        return (
            remote(own, field.at[pl.ds(0, rows)], h2_send.at[c, o, 0], h2_recv.at[c, o, 0], right),
            remote(
                own, field.at[pl.ds(2 * rows, rows)], h2_send.at[c, o, 1], h2_recv.at[c, o, 1], left
            ),
        )

    class Gather:
        def __init__(self, z, n, relay):
            self.z, self.n = z, n
            self.relay = relay and planes % 2 == 0 and planes > 2

        def slot(self, k, a, b):
            return self.z.at[k, a, b]

        def row(self, k, a):
            return self.z.at[k, a]

        def across(self, t):
            part = self.slot(core, plane, place)
            peer = device_at(plane, (place + t) % inner, core)
            return remote(part, part, y_send.at[self.n, t], y_recv.at[self.n, t], peer)

        def along(self, t):
            to = (plane + t) % planes
            part = self.row(core, plane)
            return remote(
                part,
                part,
                r_send.at[self.n, t],
                r_recv.at[self.n, plane],
                device_at(to, place, core),
            )

        def goes(self, t):
            if not self.relay:
                return None
            to = (plane + t) % planes
            mine = plane // half
            other = jnp.where(mine == 0, half, half - 1)
            return (to // half == mine) | (to == other)

        def arrival(self, source):
            part = self.row(core, source)
            return remote(part, part, r_send.at[self.n, 0], r_recv.at[self.n, source], partner)

        def passing(self, source, i, t):
            mine = plane // half
            to = mine * half + (plane % half + t) % half
            part = self.row(core, source)
            return remote(
                part,
                part,
                q_send.at[self.n, i, t],
                r_recv.at[self.n, source],
                device_at(to, place, core),
            )

        def is_entry(self):
            return jnp.where(plane < half, half - 1, half) == plane

        def forward(self, source):
            part = self.row(core, source)
            return remote(part, part, f_send.at[self.n, source], f_recv.at[self.n, source], partner)

        def start(self):
            for t in range(1, inner):
                self.across(t).start()

        def rowwise(self):
            for t in range(1, inner):
                self.across(t).wait_recv()
            for t in range(1, planes):
                go = self.goes(t)
                if go is None:
                    self.along(t).start()
                else:
                    pl.when(go)(lambda t=t: self.along(t).start())
            self.forward(plane).start()

        def hand_on(self):
            if not self.relay:
                return
            self.each_pass(True)

        def each_pass(self, starts):
            first = jnp.where(plane < half, half, 0)

            @pl.when(self.is_entry())
            def _():
                for i in range(half):
                    if starts:
                        self.arrival(first + i).wait_recv()
                    for t in range(1, half):
                        copy = self.passing(first + i, i, t)
                        if starts:
                            copy.start()
                        else:
                            copy.wait_send()

        def finish(self):
            for t in range(1, planes):
                source = (plane + t) % planes
                if self.relay:
                    taken = self.is_entry() & (source // half != plane // half)
                    pl.when(jnp.logical_not(taken))(
                        lambda source=source: self.arrival(source).wait_recv()
                    )
                else:
                    self.arrival(source).wait_recv()
                self.forward(source).start()
            for t in range(planes):
                self.forward((plane + t) % planes).wait_recv()

        def drain(self):
            for t in range(1, inner):
                self.across(t).wait_send()
            for t in range(1, planes):
                go = self.goes(t)
                if go is None:
                    self.along(t).wait_send()
                else:
                    pl.when(go)(lambda t=t: self.along(t).wait_send())
            for t in range(planes):
                self.forward((plane + t) % planes).wait_send()
            if self.relay:
                self.each_pass(False)

    gather1 = [Gather(z1[c], c, RELAY1[min(c, len(RELAY1) - 1)]) for c in range(chunks)]
    gather2 = [Gather(z2[c], chunks + c, True) for c in range(chunks)]

    def to_coeffs(r, values):
        return jnp.dot(right_ref[r], values, preferred_element_type=F32).astype(BF16)

    for c in range(chunks):
        for copy in halo1(c):
            copy.start()
    loads[0].wait()
    for c in range(chunks):
        own_copy(c).wait()
        for r in range(local):
            value = to_coeffs(r, u1[c, pl.ds(rows + r * size, size)])
            z1[c][core, plane, place, pl.ds(r * pieces, pieces)] = value.reshape(
                pieces, GROUP, width
            )
        gather1[c].start()
    for load in loads[1:]:
        load.wait()

    def prepare(r):
        row = me * local + r
        for d in range(near):
            target = (row + d - REACH + blocks) % blocks
            slot = jnp.int32(0)
            for k in range(1, near):
                slot = jnp.where(cols_ref[r, k] == target, k, slot)
            live = (slot < count_ref[r]).astype(F32).astype(BF16)
            for o in range(2):
                w_ref[r, pl.ds(o * size, size), pl.ds(d * size, size)] = (
                    tiles_ref[o, r, slot] * live
                )
        for o in range(2):
            parts = [
                lax.dot_general(
                    coup_ref[o, r, k],
                    left_ref[r],
                    (((0,), (0,)), ((), ())),
                    preferred_element_type=F32,
                )
                for k in range(far)
            ]
            if g_ref.shape[2] > far * rank:
                parts.append(jnp.zeros((g_ref.shape[2] - far * rank, size), F32))
            g_ref[r, pl.ds(o * size, size)] = jnp.concatenate(parts, axis=0).T.astype(BF16)
        diag = lax.broadcasted_iota(jnp.int32, (size, size), 0) == lax.broadcasted_iota(
            jnp.int32, (size, size), 1
        )
        for o in range(2):
            line = self_ref[pl.ds(o, 1), pl.ds(r * size, size)]
            self_col[o, pl.ds(r * size, size)] = jnp.sum(
                jnp.where(diag, line, 0.0), axis=1, keepdims=True
            )

    prepare(0)
    for c in range(chunks):
        gather1[c].rowwise()
    for r in range(1, local):
        prepare(r)
    zsel[...] = jnp.zeros_like(zsel)

    def where_is(block):
        owner = block // local
        return owner % CORES, owner // CORES // inner, owner // CORES % inner, block % local

    def first(c):
        for copy in halo1(c):
            copy.wait_recv()
        for r in range(local):
            total = jnp.dot(
                w_ref[r],
                u1[c, pl.ds(r * size, near * size)],
                preferred_element_type=F32,
            )
            for o in range(2):
                y_ref[o, pl.ds(r * size, size)] = total[o * size : (o + 1) * size]
        gather1[c].hand_on()
        gather1[c].finish()
        for r in range(local):
            for k in range(far):
                k_core, a, b, which = where_is(far_ref[r, k])
                zsel[r, pl.ds(k * rank, rank)] = z1[c][
                    k_core, a, b, pl.ds(which * pieces, pieces)
                ].reshape(rank, width)
        q = jnp.zeros((1, width), F32)
        p = [jnp.zeros((1, width), F32) for _ in range(2)]
        for r in range(local):
            more = jnp.dot(g_ref[r], zsel[r], preferred_element_type=F32)
            own = u1[c, pl.ds(rows + r * size, size)].astype(F32)
            q += jnp.sum(own * own, axis=0, keepdims=True)
            for o in range(2):
                at = pl.ds(r * size, size)
                value = y_ref[o, at] + more[o * size : (o + 1) * size] + self_col[o, at] * own
                y_ref[o, at] = value
                p[o] += jnp.sum(value * own, axis=0, keepdims=True)
        h = [p[o] / jnp.maximum(q, TINY) for o in range(2)]
        rest = []
        own = u1[c, pl.ds(rows, rows)].astype(F32)
        for o in range(2):
            rem = y_ref[o] - h[o] * own
            rest.append(jnp.sum(rem * rem, axis=0, keepdims=True))
            value = rem.astype(BF16)
            u2[c, o, pl.ds(rows, rows)] = value
            for r in range(local):
                z2[c][core, plane, place, pl.ds((r * 2 + o) * pieces, pieces)] = to_coeffs(
                    r, value[r * size : (r + 1) * size]
                ).reshape(pieces, GROUP, width)
        lines = []
        for x in (q, *h, *rest):
            lines += split3(x)
        lines.append(jnp.zeros((GROUP - len(lines), width), F32))
        z2[c][core, plane, place, 2 * local * pieces] = jnp.concatenate(lines, axis=0).astype(BF16)
        gather2[c].start()
        for o in range(2):
            for copy in halo2(c, o):
                copy.start()

    def stat(tile, i):
        part = tile[..., 3 * i : 3 * i + 1, :]
        return (
            part
            + tile[..., 3 * i + 1 : 3 * i + 2, :]
            + tile[..., 3 * i + 2 : 3 * i + 3, :]
        )

    def stat_at(c, device):
        k, a, b = device % CORES, device // CORES // inner, device // CORES % inner
        return z2[c][k, a, b, 2 * local * pieces].astype(F32)

    def third(c):
        cut = pl.ds(c * width, width)
        every = z2[c][:, :, :, 2 * local * pieces].astype(F32).reshape(devices, GROUP, width)
        q = stat(every, 0)
        scale = jnp.sum(q, axis=0) / panels
        inv = 1.0 / jnp.sqrt(scale + EPSILON)
        lines = [stat_at(c, left), stat_at(c, me), stat_at(c, right)]
        outs = []
        for o in range(2):
            local_h = stat(every, 1 + o)
            raw = jnp.sum(local_h * q, axis=0)
            h = raw * inv * inv / panels
            off = local_h - h[None]
            spread = jnp.sum(stat(every, 3 + o) + off * off * q, axis=0) * inv * inv / panels
            norm = jnp.sqrt(spread + EPSILON)
            heights_ref[pl.ds(o, 1), cut] = h
            norms_ref[pl.ds(o, 1), cut] = norm
            factor = inv / norm
            for copy in halo2(c, o):
                copy.wait_recv()
            for i, line in enumerate(lines):
                at = pl.ds(i * rows, rows)
                delta = stat(line, 1 + o) - h
                uw[at] = (u2[c, o, at].astype(F32) + delta * u1[c, at].astype(F32)).astype(BF16)
            for r in range(local):
                for k in range(far):
                    k_core, a, b, which = where_is(far_ref[r, k])
                    coeffs = z2[c][
                        k_core, a, b, pl.ds((which * 2 + o) * pieces, pieces)
                    ].reshape(rank, width)
                    base = z1[c][k_core, a, b, pl.ds(which * pieces, pieces)].reshape(rank, width)
                    line = z2[c][k_core, a, b, 2 * local * pieces].astype(F32)
                    delta = stat(line, 1 + o) - h
                    zsel[r, pl.ds(k * rank, rank)] = (
                        coeffs.astype(F32) + delta * base.astype(F32)
                    ).astype(BF16)
                at = pl.ds(r * size, size)
                total = jnp.dot(
                    w_ref[r, pl.ds(o * size, size)],
                    uw[pl.ds(r * size, near * size)],
                    preferred_element_type=F32,
                )
                total += jnp.dot(
                    g_ref[r, pl.ds(o * size, size)], zsel[r], preferred_element_type=F32
                )
                own = uw[pl.ds(rows + r * size, size)].astype(F32)
                out_ref[o, at, cut] = (total + self_col[o, at] * own) * factor
            copy_out(c, o).start()

    def copy_out(c, o):
        cut = pl.ds(c * width, width)
        return pltpu.make_async_copy(out_ref.at[o, :, cut], out_any.at[o, :, cut], out_sem.at[c, o])

    for c in range(chunks):
        first(c)
        if c >= 1:
            gather2[c - 1].rowwise()
        if c >= 2:
            gather2[c - 2].hand_on()
            gather2[c - 2].finish()
    for c in range(max(chunks - 2, 0), chunks):
        if c == chunks - 1:
            gather2[c].rowwise()
        gather2[c].hand_on()
        gather2[c].finish()
    for c in range(chunks):
        third(c)

    small = (
        pltpu.make_async_copy(heights_ref, heights_any, in_sem.at[0]),
        pltpu.make_async_copy(norms_ref, norms_any, in_sem.at[1]),
    )
    for copy in small:
        copy.start()
    for c in range(chunks):
        for copy in halo1(c):
            copy.wait_send()
        for o in range(2):
            for copy in halo2(c, o):
                copy.wait_send()
        gather1[c].drain()
        gather2[c].drain()
    for copy in small:
        copy.wait()
    for c in range(chunks):
        for o in range(2):
            copy_out(c, o).wait()


def hand_over(images_ref, heights_ref, norms_ref, out_images, out_heights, out_norms, sem):
    copies = [
        pltpu.make_async_copy(a, b, sem.at[i])
        for i, (a, b) in enumerate(
            (
                (images_ref, out_images),
                (heights_ref, out_heights),
                (norms_ref, out_norms),
            )
        )
    ]
    for copy in copies:
        copy.start()
    for copy in copies:
        copy.wait()


def shards(
    devices,
    sources,
    self_terms,
    near_tiles,
    near_cols,
    near_count,
    far_cols,
    basis_left,
    basis_right,
    couplings,
):
    rows, columns = sources.shape
    local, near, size = near_tiles.shape[1:4]
    far, rank = couplings.shape[2:4]
    chunks = columns // CHUNK
    planes, inner = grid_of(devices)
    depth = -(-far * rank // 128) * 128
    pieces = rank // GROUP
    dma = pltpu.SemaphoreType.DMA
    smem = pl.BlockSpec(memory_space=pltpu.SMEM)
    hbm = pl.BlockSpec(memory_space=pltpu.HBM)
    anywhere = pl.BlockSpec(memory_space=pl.ANY)
    moved = devices * (3 * local * rank + GROUP) * columns * 2
    gathers = 2 * chunks
    results = pl.pallas_call(
        functools.partial(kernel, devices),
        out_shape=(
            jax.ShapeDtypeStruct((2, rows, columns), F32),
            jax.ShapeDtypeStruct((2, columns), F32),
            jax.ShapeDtypeStruct((2, columns), F32),
        ),
        in_specs=[smem] * 3 + [hbm] * 6,
        out_specs=(anywhere,) * 3,
        scratch_shapes=[
            pltpu.VMEM(self_terms.shape, F32),
            pltpu.VMEM(near_tiles.shape, BF16),
            pltpu.VMEM((local, rank, size), BF16),
            pltpu.VMEM((local, rank, size), BF16),
            pltpu.VMEM(couplings.shape, BF16),
            pltpu.VMEM((2, rows, columns), F32),
            pltpu.VMEM((2, columns), F32),
            pltpu.VMEM((2, columns), F32),
            pltpu.VMEM((local, 2 * size, near * size), BF16),
            pltpu.VMEM((local, 2 * size, depth), BF16),
            pltpu.VMEM((2, rows, 1), F32),
            pltpu.VMEM((chunks, 3 * rows, CHUNK), BF16),
            pltpu.VMEM((chunks, 2, 3 * rows, CHUNK), BF16),
            pltpu.VMEM((3 * rows, CHUNK), BF16),
            [pltpu.VMEM((CORES, planes, inner, local * pieces, GROUP, CHUNK), BF16)] * chunks,
            [pltpu.VMEM((CORES, planes, inner, 2 * local * pieces + 1, GROUP, CHUNK), BF16)]
            * chunks,
            pltpu.VMEM((local, depth, CHUNK), BF16),
            pltpu.VMEM((2, rows, CHUNK), F32),
            dma((5,)),
            dma((chunks,)),
            dma((chunks, 2)),
            dma((chunks, 2)),
            dma((chunks, 2)),
            dma((chunks, 2, 2)),
            dma((chunks, 2, 2)),
            dma((gathers, inner)),
            dma((gathers, inner)),
            dma((gathers, planes)),
            dma((gathers, planes)),
            dma((gathers, max(planes // 2, 1), max(planes // 2, 1))),
            dma((gathers, planes)),
            dma((gathers, planes)),
        ],
        compiler_params=pltpu.CompilerParams(
            collective_id=0, has_side_effects=True, vmem_limit_bytes=24 * 1024 * 1024 + moved
        ),
    )(
        *(
            pltpu.with_memory_space_constraint(x, pltpu.HBM)
            for x in (
                near_cols,
                near_count,
                far_cols,
                sources,
                self_terms,
                near_tiles,
                jnp.swapaxes(basis_left, 1, 2),
                jnp.swapaxes(basis_right, 1, 2),
                couplings,
            )
        )
    )
    return pl.pallas_call(
        hand_over,
        out_shape=tuple(jax.ShapeDtypeStruct(r.shape, r.dtype) for r in results),
        in_specs=(anywhere,) * 3,
        out_specs=(anywhere,) * 3,
        scratch_shapes=[dma((3,))],
        compiler_params=pltpu.CompilerParams(vmem_limit_bytes=1024 * 1024),
    )(*results)


def solution(mesh):
    placed = (
        P(("groups", "store"), None),
        P(None, "store"),
        P(None, "store", None, None, None),
        P("store", None),
        P("store"),
        P("store", None),
        P("store", None, None),
        P("store", None, None),
        P(None, "store", None, None, None),
    )
    return jax.shard_map(
        functools.partial(shards, mesh.shape["store"]),
        mesh=mesh,
        in_specs=placed,
        out_specs=(P(None, ("groups", "store"), None), P("groups", None), P("groups", None)),
        check_vma=False,
    )
```

```python
import functools

import jax
import jax.numpy as jnp
from jax import lax
from jax.experimental import pallas as pl
from jax.experimental.pallas import tpu as pltpu
from jax.sharding import PartitionSpec as P

REACH = 2
EPSILON = 1e-06
CHUNK = 128
GROUP = 16
STATS = 3
CORES = 2
TINY = 1e-30
MESH = pl.DeviceIdType.MESH
F32 = jnp.float32
BF16 = jnp.bfloat16


def grid_of(devices):
    chips = devices // CORES
    inner = 1
    while inner * inner * 4 <= chips:
        inner *= 2
    return chips // inner, inner


def chunks_of(columns):
    return columns // CHUNK


def split3(x):
    high = x.astype(BF16)
    rest = x - high.astype(F32)
    mid = rest.astype(BF16)
    low = (rest - mid.astype(F32)).astype(BF16)
    return [high.astype(F32), mid.astype(F32), low.astype(F32)]


def kernel(
    devices,
    cols_ref,
    count_ref,
    far_ref,
    src_hbm,
    self_hbm,
    tiles_hbm,
    left_hbm,
    right_hbm,
    coup_hbm,
    out_any,
    heights_any,
    norms_any,
    self_ref,
    tiles_ref,
    left_ref,
    right_ref,
    coup_ref,
    out_ref,
    heights_ref,
    norms_ref,
    w_ref,
    left_t,
    self_col,
    u1,
    u2,
    uw,
    y_ref,
    zo1,
    zo2,
    zi1,
    zi2,
    zc,
    zsel,
    cm,
    fv,
    fs,
    co1,
    co2,
    ci1,
    ci2,
    in_sem,
    src_sem,
    out_sem,
    fs_sem,
    own_sem,
    h1_send,
    h1_recv,
    h2_send,
    h2_recv,
    m_send,
    m_recv,
    n_send,
    n_recv,
    z_send,
    z_recv,
    y_send,
    y_recv,
    f_send,
    f_recv,
    c_send,
    c_recv,
):
    me = lax.axis_index("store")
    planes, inner = grid_of(devices)
    chips = devices // CORES
    chip = me // CORES
    core = me % CORES
    plane = chip // inner
    place = chip % inner
    homes = planes // chunks_of(src_hbm.shape[1])
    partner = chip * CORES + (1 - core)
    right = (me + 1) % devices
    left = (me + devices - 1) % devices
    local, near, size = tiles_ref.shape[1:4]
    far, rank = coup_ref.shape[2:4]
    rows = local * size
    width = u1.shape[2]
    chunks = u1.shape[0]
    blocks = devices * local
    panels = blocks * size
    pieces = rank // GROUP

    def device_at(a, b, k):
        return (a * inner + b) * CORES + k

    def remote(src, dst, send, recv, peer):
        return pltpu.make_async_remote_copy(
            src_ref=src,
            dst_ref=dst,
            send_sem=send,
            recv_sem=recv,
            device_id={"store": peer},
            device_id_type=MESH,
        )

    barrier = pltpu.get_barrier_semaphore()

    def greet(peer):
        pl.semaphore_signal(barrier, inc=1, device_id={"store": peer}, device_id_type=MESH)

    greet(left)
    greet(right)
    for t in range(1, inner):
        to = (place + t) % inner
        greet(device_at(plane, to, core))
    for t in range(1, planes):
        greet(device_at((plane + t) % planes, place, core))

    def own_copy(c):
        return pltpu.make_async_copy(
            src_hbm.at[:, pl.ds(c * width, width)],
            u1.at[c, pl.ds(rows, rows)],
            src_sem.at[c],
        )

    loads = [
        pltpu.make_async_copy(hbm, vmem, in_sem.at[i])
        for i, (hbm, vmem) in enumerate(
            (
                (right_hbm, right_ref),
                (tiles_hbm, tiles_ref),
                (left_hbm, left_ref),
                (coup_hbm, coup_ref),
                (self_hbm, self_ref),
            )
        )
    ]
    loads[0].start()
    for c in range(chunks):
        own_copy(c).start()
    for load in loads[1:]:
        load.start()

    def halo1(c):
        own = src_hbm.at[:, pl.ds(c * width, width)]
        return (
            remote(own, u1.at[c, pl.ds(0, rows)], h1_send.at[c, 0], h1_recv.at[c, 0], right),
            remote(own, u1.at[c, pl.ds(2 * rows, rows)], h1_send.at[c, 1], h1_recv.at[c, 1], left),
        )

    def halo2(c, o):
        field = u2.at[c, o]
        own = field.at[pl.ds(rows, rows)]
        return (
            remote(own, field.at[pl.ds(0, rows)], h2_send.at[c, o, 0], h2_recv.at[c, o, 0], right),
            remote(
                own, field.at[pl.ds(2 * rows, rows)], h2_send.at[c, o, 1], h2_recv.at[c, o, 1], left
            ),
        )

    def home(c):
        return c * homes

    has_home = plane % homes == 0
    mine = plane // homes
    groups = local * 2 * pieces

    class Stage:
        def __init__(self, n, zo, zi, co, ci):
            self.n, self.zo, self.zi, self.co, self.ci = n, zo, zi, co, ci

        def give_copy(self, c):
            return remote(
                self.zo.at[c],
                self.zi.at[place, core, plane],
                z_send.at[self.n, c],
                z_recv.at[self.n, plane],
                device_at(home(c), place, core),
            )

        def give(self, c):
            @pl.when(plane == home(c))
            def _():
                self.zi[place, core, plane] = self.zo[c]

            @pl.when(plane != home(c))
            def _():
                self.give_copy(c).start()

        def got(self, source):
            part = self.zi.at[place, core, source]
            return remote(part, part, z_send.at[self.n, 0], z_recv.at[self.n, source], partner)

        def across(self, t):
            part = self.zi.at[place, core]
            return remote(
                part,
                part,
                y_send.at[self.n, t],
                y_recv.at[self.n, place],
                device_at(plane, (place + t) % inner, core),
            )

        def crossed(self, source):
            part = self.zi.at[source, core]
            return remote(part, part, y_send.at[self.n, 0], y_recv.at[self.n, source], partner)

        def forward(self, source):
            part = self.zi.at[source, core]
            return remote(part, part, f_send.at[self.n, source], f_recv.at[self.n, source], partner)

        def spread(self):
            @pl.when(has_home)
            def _():
                for t in range(1, planes):
                    self.got((plane + t) % planes).wait_recv()
                for t in range(1, inner):
                    self.across(t).start()
                self.forward(place).start()

        def share(self):
            @pl.when(has_home)
            def _():
                for t in range(1, inner):
                    source = (place + t) % inner
                    self.crossed(source).wait_recv()
                    self.forward(source).start()

        def complete(self):
            @pl.when(has_home)
            def _():
                for b in range(inner):
                    part = self.zi.at[b, 1 - core]
                    remote(
                        part, part, f_send.at[self.n, b], f_recv.at[self.n, b], partner
                    ).wait_recv()

        def back_copy(self, p):
            return remote(
                self.co.at[p],
                self.ci.at[mine],
                c_send.at[self.n, p],
                c_recv.at[self.n, mine],
                device_at(p, place, core),
            )

        def give_back(self):
            @pl.when(has_home)
            def _():
                own = pltpu.make_async_copy(
                    self.co.at[plane], self.ci.at[mine], own_sem.at[self.n]
                )
                own.start()
                for t in range(1, planes):
                    self.back_copy((plane + t) % planes).start()
                own.wait()

        def back(self, c):
            @pl.when(plane != home(c))
            def _():
                part = self.ci.at[c]
                remote(
                    part, part, c_send.at[self.n, 0], c_recv.at[self.n, c], partner
                ).wait_recv()

        def drain(self):
            for c in range(chunks):
                pl.when(plane != home(c))(lambda c=c: self.give_copy(c).wait_send())

            @pl.when(has_home)
            def _():
                for t in range(1, inner):
                    self.across(t).wait_send()
                for b in range(inner):
                    self.forward(b).wait_send()
                for t in range(1, planes):
                    self.back_copy((plane + t) % planes).wait_send()

    stage1 = Stage(0, zo1, zi1, co1, ci1)
    stage2 = Stage(1, zo2, zi2, co2, ci2)

    def to_coeffs(r, values):
        return (
            jnp.dot(right_ref[r], values, preferred_element_type=F32)
            .astype(BF16)
            .reshape(pieces, GROUP, width)
        )

    def table_copies(t):
        to = device_at((plane + t) % planes, place, core)
        m, n = cm.at[plane], fv.at[plane]
        return (
            remote(n, n, n_send.at[t], n_recv.at[plane], to),
            remote(m, m, m_send.at[t], m_recv.at[plane], to),
        )

    def table_waits(t):
        source = (plane + t) % planes
        m, n = cm.at[source], fv.at[source]
        return (
            remote(n, n, n_send.at[t], n_recv.at[source], partner),
            remote(m, m, m_send.at[t], m_recv.at[source], partner),
        )

    def start1(c):
        if c < chunks:
            for copy in halo1(c):
                copy.start()

    loads[0].wait()
    for c in range(chunks):
        own_copy(c).wait()
        for r in range(local):
            value = to_coeffs(r, u1[c, pl.ds(rows + r * size, size)])
            zo1[c, pl.ds(r * pieces, pieces)] = value
    for load in loads[1:]:
        load.wait()
    line = lax.broadcasted_iota(jnp.int32, (8, 128), 0)
    lane = lax.broadcasted_iota(jnp.int32, (8, 128), 1)
    table = jnp.zeros((8, 128), jnp.int32)
    for r in range(local):
        for k in range(far):
            table = jnp.where((line == r) & (lane == k), far_ref[r, k], table)
        for o in range(2):
            parts = [coup_ref[o, r, k] for k in range(far)]
            if cm.shape[3] > far * rank:
                parts.append(jnp.zeros((rank, cm.shape[3] - far * rank), BF16))
            cm[plane, r, pl.ds(o * rank, rank)] = jnp.concatenate(parts, axis=1)
    fv[plane] = table

    pl.semaphore_wait(barrier, 2 + inner - 1 + planes - 1)

    for c in range(chunks):
        stage1.give(c)
    start1(0)
    for t in range(1, planes):
        for copy in table_copies(t):
            copy.start()

    def prepare(r):
        row = me * local + r
        for d in range(near):
            target = (row + d - REACH + blocks) % blocks
            slot = jnp.int32(0)
            for k in range(1, near):
                slot = jnp.where(cols_ref[r, k] == target, k, slot)
            live = (slot < count_ref[r]).astype(F32).astype(BF16)
            for o in range(2):
                w_ref[r, pl.ds(o * size, size), pl.ds(d * size, size)] = (
                    tiles_ref[o, r, slot] * live
                )
        left_t[r] = left_ref[r].astype(F32).T.astype(BF16)
        diag = lax.broadcasted_iota(jnp.int32, (size, size), 0) == lax.broadcasted_iota(
            jnp.int32, (size, size), 1
        )
        for o in range(2):
            line = self_ref[pl.ds(o, 1), pl.ds(r * size, size)]
            self_col[o, pl.ds(r * size, size)] = jnp.sum(
                jnp.where(diag, line, 0.0), axis=1, keepdims=True
            )

    zsel[...] = jnp.zeros_like(zsel)
    prepare(0)

    def where_is(device):
        return device // CORES % inner, device % CORES, device // CORES // inner

    def chosen(z, p, r, k, scale, o):
        block = fs[p, r, k]
        at = (block % local * scale + o) * pieces
        return z[(*where_is(block // local), pl.ds(at, pieces))].reshape(rank, width)

    def sums1():
        @pl.when(has_home)
        def _():
            for p in range(planes):
                for r in range(local):
                    for k in range(far):
                        zsel[0, pl.ds(k * rank, rank)] = chosen(zi1, p, r, k, 1, 0)
                    value = jnp.dot(cm[p, r], zsel[0], preferred_element_type=F32)
                    co1[p, pl.ds(r * 2 * pieces, 2 * pieces)] = value.astype(BF16).reshape(
                        2 * pieces, GROUP, width
                    )

    def stat(tile, i):
        part = tile[..., 3 * i : 3 * i + 1, :]
        return (
            part
            + tile[..., 3 * i + 1 : 3 * i + 2, :]
            + tile[..., 3 * i + 2 : 3 * i + 3, :]
        )

    def sums2():
        @pl.when(has_home)
        def _():
            every = zi2[:, :, :, groups].astype(F32).reshape(devices, GROUP, width)
            q = stat(every, 0)
            scale = jnp.sum(q, axis=0) / panels
            inv = 1.0 / jnp.sqrt(scale + EPSILON)
            totals = []
            for o in range(2):
                local_h = stat(every, 1 + o)
                h = jnp.sum(local_h * q, axis=0) * inv * inv / panels
                off = local_h - h[None]
                spread = jnp.sum(stat(every, 3 + o) + off * off * q, axis=0) * inv * inv / panels
                norm = jnp.sqrt(spread + EPSILON)
                totals.append((inv / norm, h, norm))
                delta = off.reshape(inner, CORES, planes, 1, 1, width)
                for r in range(local):
                    at = pl.ds((r * 2 + o) * pieces, pieces)
                    base = zi1[:, :, :, pl.ds(r * pieces, pieces)].astype(F32)
                    zc[:, :, :, at] = (zi2[:, :, :, at].astype(F32) + delta * base).astype(BF16)
            for p in range(planes):
                for r in range(local):
                    for o in range(2):
                        for k in range(far):
                            zsel[o, pl.ds(k * rank, rank)] = chosen(zc, p, r, k, 2, o)
                        value = jnp.dot(
                            cm[p, r, pl.ds(o * rank, rank)],
                            zsel[o],
                            preferred_element_type=F32,
                        )
                        co2[p, pl.ds((r * 2 + o) * pieces, pieces)] = value.astype(BF16).reshape(
                            pieces, GROUP, width
                        )
                target = device_at(p, place, core)
                lines = []
                for o in range(2):
                    for shift in (devices - 1, 0, 1):
                        tile = zi2[(*where_is((target + shift) % devices), groups)].astype(F32)
                        lines += split3(stat(tile, 1 + o) - totals[o][1])
                    for x in totals[o]:
                        lines += split3(x)
                lines.append(jnp.zeros((STATS * GROUP - len(lines), width), F32))
                co2[p, pl.ds(groups, STATS)] = (
                    jnp.concatenate(lines, axis=0).astype(BF16).reshape(STATS, GROUP, width)
                )

    def first(c):
        for copy in halo1(c):
            copy.wait_recv()
        for r in range(local):
            total = jnp.dot(
                w_ref[r],
                u1[c, pl.ds(r * size, near * size)],
                preferred_element_type=F32,
            )
            for o in range(2):
                y_ref[c, o, pl.ds(r * size, size)] = total[o * size : (o + 1) * size]

    def second(c):
        stage1.back(c)
        q = jnp.zeros((1, width), F32)
        p = [jnp.zeros((1, width), F32) for _ in range(2)]
        for r in range(local):
            own = u1[c, pl.ds(rows + r * size, size)].astype(F32)
            q += jnp.sum(own * own, axis=0, keepdims=True)
            for o in range(2):
                at = pl.ds(r * size, size)
                coeffs = ci1[c, pl.ds((r * 2 + o) * pieces, pieces)].reshape(rank, width)
                more = jnp.dot(left_t[r], coeffs, preferred_element_type=F32)
                value = y_ref[c, o, at] + more + self_col[o, at] * own
                y_ref[c, o, at] = value
                p[o] += jnp.sum(value * own, axis=0, keepdims=True)
        h = [p[o] / jnp.maximum(q, TINY) for o in range(2)]
        rest = []
        own = u1[c, pl.ds(rows, rows)].astype(F32)
        for o in range(2):
            rem = y_ref[c, o] - h[o] * own
            rest.append(jnp.sum(rem * rem, axis=0, keepdims=True))
            value = rem.astype(BF16)
            u2[c, o, pl.ds(rows, rows)] = value
            for r in range(local):
                zo2[c, pl.ds((r * 2 + o) * pieces, pieces)] = to_coeffs(
                    r, value[r * size : (r + 1) * size]
                )
        lines = []
        for x in (q, *h, *rest):
            lines += split3(x)
        lines.append(jnp.zeros((GROUP - len(lines), width), F32))
        zo2[c, groups] = jnp.concatenate(lines, axis=0).astype(BF16)
        stage2.give(c)

    def third(c):
        cut = pl.ds(c * width, width)
        stage2.back(c)
        told = ci2[c, pl.ds(groups, STATS)].astype(F32).reshape(STATS * GROUP, width)
        for o in range(2):
            factor, h, norm = (stat(told, 6 * o + i) for i in range(3, 6))
            heights_ref[pl.ds(o, 1), cut] = h
            norms_ref[pl.ds(o, 1), cut] = norm
            for copy in halo2(c, o):
                copy.wait_recv()
            for i in range(3):
                at = pl.ds(i * rows, rows)
                delta = stat(told, 6 * o + i)
                uw[at] = (u2[c, o, at].astype(F32) + delta * u1[c, at].astype(F32)).astype(BF16)
            for r in range(local):
                at = pl.ds(r * size, size)
                coeffs = ci2[c, pl.ds((r * 2 + o) * pieces, pieces)].reshape(rank, width)
                total = jnp.dot(
                    w_ref[r, pl.ds(o * size, size)],
                    uw[pl.ds(r * size, near * size)],
                    preferred_element_type=F32,
                )
                total += jnp.dot(left_t[r], coeffs, preferred_element_type=F32)
                own = uw[pl.ds(rows + r * size, size)].astype(F32)
                out_ref[o, at, cut] = (total + self_col[o, at] * own) * factor
            copy_out(c, o).start()

    def copy_out(c, o):
        cut = pl.ds(c * width, width)
        return pltpu.make_async_copy(out_ref.at[o, :, cut], out_any.at[o, :, cut], out_sem.at[c, o])

    sent = []

    def send(count):
        for _ in range(count):
            n = len(sent)
            if n < 2 * chunks:
                sent.append(n)
                for copy in halo2(n // 2, n % 2):
                    copy.start()

    stage1.spread()
    start1(1)
    for r in range(1, local):
        prepare(r)
    stage1.share()
    start1(2)
    for t in range(1, planes):
        for copy in table_waits(t):
            copy.wait_recv()
    index = pltpu.make_async_copy(fv, fs, fs_sem)
    index.start()
    stage1.complete()
    index.wait()
    sums1()
    stage1.give_back()
    for c in range(3, chunks):
        start1(c)
    first(0)
    for c in range(chunks):
        second(c)
        if c < 2:
            send(2 - c)
        if c + 1 < chunks:
            first(c + 1)
    stage2.spread()
    send(2)
    stage2.share()
    send(1)
    stage2.complete()
    sums2()
    stage2.give_back()
    send(2 * chunks)
    for c in range(chunks):
        third(c)

    small = (
        pltpu.make_async_copy(heights_ref, heights_any, in_sem.at[0]),
        pltpu.make_async_copy(norms_ref, norms_any, in_sem.at[1]),
    )
    for copy in small:
        copy.start()
    for c in range(chunks):
        for copy in halo1(c):
            copy.wait_send()
        for o in range(2):
            for copy in halo2(c, o):
                copy.wait_send()
    stage1.drain()
    stage2.drain()
    for t in range(1, planes):
        for copy in table_copies(t):
            copy.wait_send()
    for copy in small:
        copy.wait()
    for c in range(chunks):
        for o in range(2):
            copy_out(c, o).wait()


def hand_over(images_ref, heights_ref, norms_ref, out_images, out_heights, out_norms, sem):
    copies = [
        pltpu.make_async_copy(a, b, sem.at[i])
        for i, (a, b) in enumerate(
            (
                (images_ref, out_images),
                (heights_ref, out_heights),
                (norms_ref, out_norms),
            )
        )
    ]
    for copy in copies:
        copy.start()
    for copy in copies:
        copy.wait()


def shards(
    devices,
    sources,
    self_terms,
    near_tiles,
    near_cols,
    near_count,
    far_cols,
    basis_left,
    basis_right,
    couplings,
):
    rows, columns = sources.shape
    local, near, size = near_tiles.shape[1:4]
    far, rank = couplings.shape[2:4]
    chunks = columns // CHUNK
    planes, inner = grid_of(devices)
    depth = -(-far * rank // 128) * 128
    pieces = rank // GROUP
    dma = pltpu.SemaphoreType.DMA
    smem = pl.BlockSpec(memory_space=pltpu.SMEM)
    hbm = pl.BlockSpec(memory_space=pltpu.HBM)
    anywhere = pl.BlockSpec(memory_space=pl.ANY)
    moved = devices * (5 * local * rank + GROUP) * CHUNK * 2
    groups = 2 * local * pieces
    results = pl.pallas_call(
        functools.partial(kernel, devices),
        out_shape=(
            jax.ShapeDtypeStruct((2, rows, columns), F32),
            jax.ShapeDtypeStruct((2, columns), F32),
            jax.ShapeDtypeStruct((2, columns), F32),
        ),
        in_specs=[smem] * 3 + [hbm] * 6,
        out_specs=(anywhere,) * 3,
        scratch_shapes=[
            pltpu.VMEM(self_terms.shape, F32),
            pltpu.VMEM(near_tiles.shape, BF16),
            pltpu.VMEM((local, rank, size), BF16),
            pltpu.VMEM((local, rank, size), BF16),
            pltpu.VMEM(couplings.shape, BF16),
            pltpu.VMEM((2, rows, columns), F32),
            pltpu.VMEM((2, columns), F32),
            pltpu.VMEM((2, columns), F32),
            pltpu.VMEM((local, 2 * size, near * size), BF16),
            pltpu.VMEM((local, size, rank), BF16),
            pltpu.VMEM((2, rows, 1), F32),
            pltpu.VMEM((chunks, 3 * rows, CHUNK), BF16),
            pltpu.VMEM((chunks, 2, 3 * rows, CHUNK), BF16),
            pltpu.VMEM((3 * rows, CHUNK), BF16),
            pltpu.VMEM((chunks, 2, rows, CHUNK), F32),
            pltpu.VMEM((chunks, groups // 2, GROUP, CHUNK), BF16),
            pltpu.VMEM((chunks, groups + 1, GROUP, CHUNK), BF16),
            pltpu.VMEM((inner, CORES, planes, groups // 2, GROUP, CHUNK), BF16),
            pltpu.VMEM((inner, CORES, planes, groups + 1, GROUP, CHUNK), BF16),
            pltpu.VMEM((inner, CORES, planes, groups, GROUP, CHUNK), BF16),
            pltpu.VMEM((2, depth, CHUNK), BF16),
            pltpu.VMEM((planes, local, 2 * rank, depth), BF16),
            pltpu.VMEM((planes, 8, 128), jnp.int32),
            pltpu.SMEM((planes, 8, 128), jnp.int32),
            pltpu.VMEM((planes, groups, GROUP, CHUNK), BF16),
            pltpu.VMEM((planes, groups + STATS, GROUP, CHUNK), BF16),
            pltpu.VMEM((chunks, groups, GROUP, CHUNK), BF16),
            pltpu.VMEM((chunks, groups + STATS, GROUP, CHUNK), BF16),
            dma((5,)),
            dma((chunks,)),
            dma((chunks, 2)),
            dma,
            dma((2,)),
            dma((chunks, 2)),
            dma((chunks, 2)),
            dma((chunks, 2, 2)),
            dma((chunks, 2, 2)),
            dma((planes,)),
            dma((planes,)),
            dma((planes,)),
            dma((planes,)),
            dma((2, chunks)),
            dma((2, planes)),
            dma((2, inner)),
            dma((2, inner)),
            dma((2, inner)),
            dma((2, inner)),
            dma((2, planes)),
            dma((2, chunks)),
        ],
        compiler_params=pltpu.CompilerParams(
            collective_id=0, has_side_effects=True, vmem_limit_bytes=28 * 1024 * 1024 + moved
        ),
    )(
        *(
            pltpu.with_memory_space_constraint(x, pltpu.HBM)
            for x in (
                near_cols,
                near_count,
                far_cols,
                sources,
                self_terms,
                near_tiles,
                jnp.swapaxes(basis_left, 1, 2),
                jnp.swapaxes(basis_right, 1, 2),
                couplings,
            )
        )
    )
    return pl.pallas_call(
        hand_over,
        out_shape=tuple(jax.ShapeDtypeStruct(r.shape, r.dtype) for r in results),
        in_specs=(anywhere,) * 3,
        out_specs=(anywhere,) * 3,
        scratch_shapes=[dma((3,))],
        compiler_params=pltpu.CompilerParams(vmem_limit_bytes=1024 * 1024),
    )(*results)


def solution(mesh):
    placed = (
        P(("groups", "store"), None),
        P(None, "store"),
        P(None, "store", None, None, None),
        P("store", None),
        P("store"),
        P("store", None),
        P("store", None, None),
        P("store", None, None),
        P(None, "store", None, None, None),
    )
    return jax.shard_map(
        functools.partial(shards, mesh.shape["store"]),
        mesh=mesh,
        in_specs=placed,
        out_specs=(P(None, ("groups", "store"), None), P("groups", None), P("groups", None)),
        check_vma=False,
    )
```

```python
import functools

import jax
import jax.numpy as jnp
from jax import lax
from jax.experimental import pallas as pl
from jax.experimental.pallas import tpu as pltpu
from jax.sharding import PartitionSpec as P

REACH = 2
EPSILON = 1e-06
CHUNK = 128
GROUP = 16
STATS = 3
PACE = (2, 1, 0, 0, 2, 2, 0)
CORES = 2
TINY = 1e-30
MESH = pl.DeviceIdType.MESH
F32 = jnp.float32
BF16 = jnp.bfloat16


def grid_of(devices):
    chips = devices // CORES
    inner = 1
    while inner * inner * 4 <= chips:
        inner *= 2
    return chips // inner, inner


def chunks_of(columns):
    return columns // CHUNK


def split3(x):
    high = x.astype(BF16)
    rest = x - high.astype(F32)
    mid = rest.astype(BF16)
    low = (rest - mid.astype(F32)).astype(BF16)
    return [high.astype(F32), mid.astype(F32), low.astype(F32)]


def kernel(
    devices,
    cols_ref,
    count_ref,
    far_ref,
    src_hbm,
    self_hbm,
    tiles_hbm,
    left_hbm,
    right_hbm,
    coup_hbm,
    out_any,
    heights_any,
    norms_any,
    self_ref,
    tiles_ref,
    left_ref,
    right_ref,
    coup_ref,
    out_ref,
    heights_ref,
    norms_ref,
    w_ref,
    left_t,
    self_col,
    u1,
    u2,
    uw,
    y_ref,
    zo1,
    zo2,
    zi1,
    zi2,
    zc,
    zsel,
    cm,
    fv,
    fs,
    co1,
    co2,
    ci1,
    ci2,
    in_sem,
    src_sem,
    out_sem,
    fs_sem,
    own_sem,
    h1_send,
    h1_recv,
    h2_send,
    h2_recv,
    m_send,
    m_recv,
    n_send,
    n_recv,
    z_send,
    z_recv,
    y_send,
    y_recv,
    f_send,
    f_recv,
    c_send,
    c_recv,
):
    me = lax.axis_index("store")
    planes, inner = grid_of(devices)
    chips = devices // CORES
    chip = me // CORES
    core = me % CORES
    plane = chip // inner
    place = chip % inner
    homes = planes // chunks_of(src_hbm.shape[1])
    partner = chip * CORES + (1 - core)
    right = (me + 1) % devices
    left = (me + devices - 1) % devices
    local, near, size = tiles_ref.shape[1:4]
    far, rank = coup_ref.shape[2:4]
    rows = local * size
    width = u1.shape[2]
    chunks = u1.shape[0]
    blocks = devices * local
    panels = blocks * size
    pieces = rank // GROUP

    def device_at(a, b, k):
        return (a * inner + b) * CORES + k

    def remote(src, dst, send, recv, peer):
        return pltpu.make_async_remote_copy(
            src_ref=src,
            dst_ref=dst,
            send_sem=send,
            recv_sem=recv,
            device_id={"store": peer},
            device_id_type=MESH,
        )

    barrier = pltpu.get_barrier_semaphore()

    def greet(peer):
        pl.semaphore_signal(barrier, inc=1, device_id={"store": peer}, device_id_type=MESH)

    greet(left)
    greet(right)
    for t in range(1, inner):
        to = (place + t) % inner
        greet(device_at(plane, to, core))
    for t in range(1, planes):
        greet(device_at((plane + t) % planes, place, core))

    def own_copy(c):
        return pltpu.make_async_copy(
            src_hbm.at[:, pl.ds(c * width, width)],
            u1.at[c, pl.ds(rows, rows)],
            src_sem.at[c],
        )

    loads = [
        pltpu.make_async_copy(hbm, vmem, in_sem.at[i])
        for i, (hbm, vmem) in enumerate(
            (
                (right_hbm, right_ref),
                (tiles_hbm, tiles_ref),
                (left_hbm, left_ref),
                (coup_hbm, coup_ref),
                (self_hbm, self_ref),
            )
        )
    ]
    loads[0].start()
    for c in range(chunks):
        own_copy(c).start()
    for load in loads[1:]:
        load.start()

    def halo1(c):
        own = src_hbm.at[:, pl.ds(c * width, width)]
        return (
            remote(own, u1.at[c, pl.ds(0, rows)], h1_send.at[c, 0], h1_recv.at[c, 0], right),
            remote(own, u1.at[c, pl.ds(2 * rows, rows)], h1_send.at[c, 1], h1_recv.at[c, 1], left),
        )

    def halo2(c, o):
        field = u2.at[c, o]
        own = field.at[pl.ds(rows, rows)]
        return (
            remote(own, field.at[pl.ds(0, rows)], h2_send.at[c, o, 0], h2_recv.at[c, o, 0], right),
            remote(
                own, field.at[pl.ds(2 * rows, rows)], h2_send.at[c, o, 1], h2_recv.at[c, o, 1], left
            ),
        )

    def home(c):
        return c * homes

    has_home = plane % homes == 0
    mine = plane // homes
    groups = local * 2 * pieces

    class Stage:
        def __init__(self, n, zo, zi, co, ci):
            self.n, self.zo, self.zi, self.co, self.ci = n, zo, zi, co, ci

        def give_copy(self, c):
            return remote(
                self.zo.at[c],
                self.zi.at[place, core, plane],
                z_send.at[self.n, c],
                z_recv.at[self.n, plane],
                device_at(home(c), place, core),
            )

        def give(self, c):
            @pl.when(plane == home(c))
            def _():
                self.zi[place, core, plane] = self.zo[c]

            @pl.when(plane != home(c))
            def _():
                self.give_copy(c).start()

        def got(self, source):
            part = self.zi.at[place, core, source]
            return remote(part, part, z_send.at[self.n, 0], z_recv.at[self.n, source], partner)

        def across(self, t):
            part = self.zi.at[place, core]
            return remote(
                part,
                part,
                y_send.at[self.n, t],
                y_recv.at[self.n, place],
                device_at(plane, (place + t) % inner, core),
            )

        def crossed(self, source):
            part = self.zi.at[source, core]
            return remote(part, part, y_send.at[self.n, 0], y_recv.at[self.n, source], partner)

        def forward(self, source):
            part = self.zi.at[source, core]
            return remote(part, part, f_send.at[self.n, source], f_recv.at[self.n, source], partner)

        def spread(self):
            @pl.when(has_home)
            def _():
                for t in range(1, planes):
                    self.got((plane + t) % planes).wait_recv()
                for t in range(1, inner):
                    self.across(t).start()
                self.forward(place).start()

        def share(self):
            @pl.when(has_home)
            def _():
                for t in range(1, inner):
                    source = (place + t) % inner
                    self.crossed(source).wait_recv()
                    self.forward(source).start()

        def complete(self):
            @pl.when(has_home)
            def _():
                for b in range(inner):
                    part = self.zi.at[b, 1 - core]
                    remote(
                        part, part, f_send.at[self.n, b], f_recv.at[self.n, b], partner
                    ).wait_recv()

        def back_copy(self, p):
            return remote(
                self.co.at[p],
                self.ci.at[mine],
                c_send.at[self.n, p],
                c_recv.at[self.n, mine],
                device_at(p, place, core),
            )

        def give_back(self):
            @pl.when(has_home)
            def _():
                own = pltpu.make_async_copy(
                    self.co.at[plane], self.ci.at[mine], own_sem.at[self.n]
                )
                own.start()
                for t in range(1, planes):
                    self.back_copy((plane + t) % planes).start()
                own.wait()

        def back(self, c):
            @pl.when(plane != home(c))
            def _():
                part = self.ci.at[c]
                remote(
                    part, part, c_send.at[self.n, 0], c_recv.at[self.n, c], partner
                ).wait_recv()

        def drain(self):
            for c in range(chunks):
                pl.when(plane != home(c))(lambda c=c: self.give_copy(c).wait_send())

            @pl.when(has_home)
            def _():
                for t in range(1, inner):
                    self.across(t).wait_send()
                for b in range(inner):
                    self.forward(b).wait_send()
                for t in range(1, planes):
                    self.back_copy((plane + t) % planes).wait_send()

    stage1 = Stage(0, zo1, zi1, co1, ci1)
    stage2 = Stage(1, zo2, zi2, co2, ci2)

    def to_coeffs(r, values):
        return (
            jnp.dot(right_ref[r], values, preferred_element_type=F32)
            .astype(BF16)
            .reshape(pieces, GROUP, width)
        )

    def table_copies(t):
        to = device_at((plane + t) % planes, place, core)
        m, n = cm.at[plane], fv.at[plane]
        return (
            remote(n, n, n_send.at[t], n_recv.at[plane], to),
            remote(m, m, m_send.at[t], m_recv.at[plane], to),
        )

    def table_waits(t):
        source = (plane + t) % planes
        m, n = cm.at[source], fv.at[source]
        return (
            remote(n, n, n_send.at[t], n_recv.at[source], partner),
            remote(m, m, m_send.at[t], m_recv.at[source], partner),
        )

    def start1(c):
        if c < chunks:
            for copy in halo1(c):
                copy.start()

    loads[0].wait()
    for c in range(chunks):
        own_copy(c).wait()
        for r in range(local):
            value = to_coeffs(r, u1[c, pl.ds(rows + r * size, size)])
            zo1[c, pl.ds(r * pieces, pieces)] = value
    pl.semaphore_wait(barrier, 2 + inner - 1 + planes - 1)

    for c in range(chunks):
        stage1.give(c)
    start1(0)
    for load in loads[1:]:
        load.wait()
    line = lax.broadcasted_iota(jnp.int32, (8, 128), 0)
    lane = lax.broadcasted_iota(jnp.int32, (8, 128), 1)
    table = jnp.zeros((8, 128), jnp.int32)
    for r in range(local):
        for k in range(far):
            table = jnp.where((line == r) & (lane == k), far_ref[r, k], table)
        for o in range(2):
            parts = [coup_ref[o, r, k] for k in range(far)]
            if cm.shape[3] > far * rank:
                parts.append(jnp.zeros((rank, cm.shape[3] - far * rank), BF16))
            cm[plane, r, pl.ds(o * rank, rank)] = jnp.concatenate(parts, axis=1)
    fv[plane] = table

    for t in range(1, planes):
        for copy in table_copies(t):
            copy.start()

    def prepare(r):
        row = me * local + r
        for d in range(near):
            target = (row + d - REACH + blocks) % blocks
            slot = jnp.int32(0)
            for k in range(1, near):
                slot = jnp.where(cols_ref[r, k] == target, k, slot)
            live = (slot < count_ref[r]).astype(F32).astype(BF16)
            for o in range(2):
                w_ref[r, pl.ds(o * size, size), pl.ds(d * size, size)] = (
                    tiles_ref[o, r, slot] * live
                )
        left_t[r] = left_ref[r].astype(F32).T.astype(BF16)
        diag = lax.broadcasted_iota(jnp.int32, (size, size), 0) == lax.broadcasted_iota(
            jnp.int32, (size, size), 1
        )
        for o in range(2):
            line = self_ref[pl.ds(o, 1), pl.ds(r * size, size)]
            self_col[o, pl.ds(r * size, size)] = jnp.sum(
                jnp.where(diag, line, 0.0), axis=1, keepdims=True
            )

    zsel[...] = jnp.zeros_like(zsel)
    prepare(0)

    def where_is(device):
        return device // CORES % inner, device % CORES, device // CORES // inner

    def chosen(z, p, r, k, scale, o):
        block = fs[p, r, k]
        at = (block % local * scale + o) * pieces
        return z[(*where_is(block // local), pl.ds(at, pieces))].reshape(rank, width)

    def sums1():
        @pl.when(has_home)
        def _():
            for p in range(planes):
                for r in range(local):
                    for k in range(far):
                        zsel[0, pl.ds(k * rank, rank)] = chosen(zi1, p, r, k, 1, 0)
                    value = jnp.dot(cm[p, r], zsel[0], preferred_element_type=F32)
                    co1[p, pl.ds(r * 2 * pieces, 2 * pieces)] = value.astype(BF16).reshape(
                        2 * pieces, GROUP, width
                    )

    def stat(tile, i):
        part = tile[..., 3 * i : 3 * i + 1, :]
        return (
            part
            + tile[..., 3 * i + 1 : 3 * i + 2, :]
            + tile[..., 3 * i + 2 : 3 * i + 3, :]
        )

    def sums2():
        @pl.when(has_home)
        def _():
            every = zi2[:, :, :, groups].astype(F32).reshape(devices, GROUP, width)
            q = stat(every, 0)
            scale = jnp.sum(q, axis=0) / panels
            inv = 1.0 / jnp.sqrt(scale + EPSILON)
            totals = []
            for o in range(2):
                local_h = stat(every, 1 + o)
                h = jnp.sum(local_h * q, axis=0) * inv * inv / panels
                off = local_h - h[None]
                spread = jnp.sum(stat(every, 3 + o) + off * off * q, axis=0) * inv * inv / panels
                norm = jnp.sqrt(spread + EPSILON)
                totals.append((inv / norm, h, norm))
                delta = off.reshape(inner, CORES, planes, 1, 1, width)
                for r in range(local):
                    at = pl.ds((r * 2 + o) * pieces, pieces)
                    base = zi1[:, :, :, pl.ds(r * pieces, pieces)].astype(F32)
                    zc[:, :, :, at] = (zi2[:, :, :, at].astype(F32) + delta * base).astype(BF16)
            for p in range(planes):
                for r in range(local):
                    for o in range(2):
                        for k in range(far):
                            zsel[o, pl.ds(k * rank, rank)] = chosen(zc, p, r, k, 2, o)
                        value = jnp.dot(
                            cm[p, r, pl.ds(o * rank, rank)],
                            zsel[o],
                            preferred_element_type=F32,
                        )
                        co2[p, pl.ds((r * 2 + o) * pieces, pieces)] = value.astype(BF16).reshape(
                            pieces, GROUP, width
                        )
                target = device_at(p, place, core)
                lines = []
                for o in range(2):
                    for shift in (devices - 1, 0, 1):
                        tile = zi2[(*where_is((target + shift) % devices), groups)].astype(F32)
                        lines += split3(stat(tile, 1 + o) - totals[o][1])
                    for x in totals[o]:
                        lines += split3(x)
                lines.append(jnp.zeros((STATS * GROUP - len(lines), width), F32))
                co2[p, pl.ds(groups, STATS)] = (
                    jnp.concatenate(lines, axis=0).astype(BF16).reshape(STATS, GROUP, width)
                )

    def first(c):
        for copy in halo1(c):
            copy.wait_recv()
        for r in range(local):
            total = jnp.dot(
                w_ref[r],
                u1[c, pl.ds(r * size, near * size)],
                preferred_element_type=F32,
            )
            for o in range(2):
                y_ref[c, o, pl.ds(r * size, size)] = total[o * size : (o + 1) * size]

    def second(c):
        stage1.back(c)
        q = jnp.zeros((1, width), F32)
        p = [jnp.zeros((1, width), F32) for _ in range(2)]
        for r in range(local):
            own = u1[c, pl.ds(rows + r * size, size)].astype(F32)
            q += jnp.sum(own * own, axis=0, keepdims=True)
            for o in range(2):
                at = pl.ds(r * size, size)
                coeffs = ci1[c, pl.ds((r * 2 + o) * pieces, pieces)].reshape(rank, width)
                more = jnp.dot(left_t[r], coeffs, preferred_element_type=F32)
                value = y_ref[c, o, at] + more + self_col[o, at] * own
                y_ref[c, o, at] = value
                p[o] += jnp.sum(value * own, axis=0, keepdims=True)
        h = [p[o] / jnp.maximum(q, TINY) for o in range(2)]
        rest = []
        own = u1[c, pl.ds(rows, rows)].astype(F32)
        for o in range(2):
            rem = y_ref[c, o] - h[o] * own
            rest.append(jnp.sum(rem * rem, axis=0, keepdims=True))
            value = rem.astype(BF16)
            u2[c, o, pl.ds(rows, rows)] = value
            for r in range(local):
                zo2[c, pl.ds((r * 2 + o) * pieces, pieces)] = to_coeffs(
                    r, value[r * size : (r + 1) * size]
                )
        lines = []
        for x in (q, *h, *rest):
            lines += split3(x)
        lines.append(jnp.zeros((GROUP - len(lines), width), F32))
        zo2[c, groups] = jnp.concatenate(lines, axis=0).astype(BF16)
        stage2.give(c)

    def third(c):
        cut = pl.ds(c * width, width)
        stage2.back(c)
        told = ci2[c, pl.ds(groups, STATS)].astype(F32).reshape(STATS * GROUP, width)
        for o in range(2):
            factor, h, norm = (stat(told, 6 * o + i) for i in range(3, 6))
            heights_ref[pl.ds(o, 1), cut] = h
            norms_ref[pl.ds(o, 1), cut] = norm
            for copy in halo2(c, o):
                copy.wait_recv()
            for i in range(3):
                at = pl.ds(i * rows, rows)
                delta = stat(told, 6 * o + i)
                uw[at] = (u2[c, o, at].astype(F32) + delta * u1[c, at].astype(F32)).astype(BF16)
            for r in range(local):
                at = pl.ds(r * size, size)
                coeffs = ci2[c, pl.ds((r * 2 + o) * pieces, pieces)].reshape(rank, width)
                total = jnp.dot(
                    w_ref[r, pl.ds(o * size, size)],
                    uw[pl.ds(r * size, near * size)],
                    preferred_element_type=F32,
                )
                total += jnp.dot(left_t[r], coeffs, preferred_element_type=F32)
                own = uw[pl.ds(rows + r * size, size)].astype(F32)
                out_ref[o, at, cut] = (total + self_col[o, at] * own) * factor
            copy_out(c, o).start()

    def copy_out(c, o):
        cut = pl.ds(c * width, width)
        return pltpu.make_async_copy(out_ref.at[o, :, cut], out_any.at[o, :, cut], out_sem.at[c, o])

    sent = []

    def send(count):
        for _ in range(count):
            n = len(sent)
            if n < 2 * chunks:
                sent.append(n)
                for copy in halo2(n // 2, n % 2):
                    copy.start()

    stage1.spread()
    start1(1)
    for r in range(1, local):
        prepare(r)
    stage1.share()
    start1(2)
    for t in range(1, planes):
        for copy in table_waits(t):
            copy.wait_recv()
    index = pltpu.make_async_copy(fv, fs, fs_sem)
    index.start()
    first(0)
    stage1.complete()
    index.wait()
    sums1()
    stage1.give_back()
    for c in range(3, chunks):
        start1(c)
    done = (0, 1)
    first(1)
    for c in range(chunks):
        second(c)
        send(PACE[min(c, 3)])
        if c + 1 < chunks and c + 1 not in done:
            first(c + 1)
    stage2.spread()
    send(PACE[4])
    stage2.share()
    send(PACE[5])
    stage2.complete()
    send(PACE[6])
    sums2()
    stage2.give_back()
    send(2 * chunks)
    for c in range(chunks):
        third(c)

    small = (
        pltpu.make_async_copy(heights_ref, heights_any, in_sem.at[0]),
        pltpu.make_async_copy(norms_ref, norms_any, in_sem.at[1]),
    )
    for copy in small:
        copy.start()
    for c in range(chunks):
        for copy in halo1(c):
            copy.wait_send()
        for o in range(2):
            for copy in halo2(c, o):
                copy.wait_send()
    stage1.drain()
    stage2.drain()
    for t in range(1, planes):
        for copy in table_copies(t):
            copy.wait_send()
    for copy in small:
        copy.wait()
    for c in range(chunks):
        for o in range(2):
            copy_out(c, o).wait()


def hand_over(images_ref, heights_ref, norms_ref, out_images, out_heights, out_norms, sem):
    copies = [
        pltpu.make_async_copy(a, b, sem.at[i])
        for i, (a, b) in enumerate(
            (
                (images_ref, out_images),
                (heights_ref, out_heights),
                (norms_ref, out_norms),
            )
        )
    ]
    for copy in copies:
        copy.start()
    for copy in copies:
        copy.wait()


def shards(
    devices,
    sources,
    self_terms,
    near_tiles,
    near_cols,
    near_count,
    far_cols,
    basis_left,
    basis_right,
    couplings,
):
    rows, columns = sources.shape
    local, near, size = near_tiles.shape[1:4]
    far, rank = couplings.shape[2:4]
    chunks = columns // CHUNK
    planes, inner = grid_of(devices)
    depth = -(-far * rank // 128) * 128
    pieces = rank // GROUP
    dma = pltpu.SemaphoreType.DMA
    smem = pl.BlockSpec(memory_space=pltpu.SMEM)
    hbm = pl.BlockSpec(memory_space=pltpu.HBM)
    anywhere = pl.BlockSpec(memory_space=pl.ANY)
    moved = devices * (5 * local * rank + GROUP) * CHUNK * 2
    groups = 2 * local * pieces
    results = pl.pallas_call(
        functools.partial(kernel, devices),
        out_shape=(
            jax.ShapeDtypeStruct((2, rows, columns), F32),
            jax.ShapeDtypeStruct((2, columns), F32),
            jax.ShapeDtypeStruct((2, columns), F32),
        ),
        in_specs=[smem] * 3 + [hbm] * 6,
        out_specs=(anywhere,) * 3,
        scratch_shapes=[
            pltpu.VMEM(self_terms.shape, F32),
            pltpu.VMEM(near_tiles.shape, BF16),
            pltpu.VMEM((local, rank, size), BF16),
            pltpu.VMEM((local, rank, size), BF16),
            pltpu.VMEM(couplings.shape, BF16),
            pltpu.VMEM((2, rows, columns), F32),
            pltpu.VMEM((2, columns), F32),
            pltpu.VMEM((2, columns), F32),
            pltpu.VMEM((local, 2 * size, near * size), BF16),
            pltpu.VMEM((local, size, rank), BF16),
            pltpu.VMEM((2, rows, 1), F32),
            pltpu.VMEM((chunks, 3 * rows, CHUNK), BF16),
            pltpu.VMEM((chunks, 2, 3 * rows, CHUNK), BF16),
            pltpu.VMEM((3 * rows, CHUNK), BF16),
            pltpu.VMEM((chunks, 2, rows, CHUNK), F32),
            pltpu.VMEM((chunks, groups // 2, GROUP, CHUNK), BF16),
            pltpu.VMEM((chunks, groups + 1, GROUP, CHUNK), BF16),
            pltpu.VMEM((inner, CORES, planes, groups // 2, GROUP, CHUNK), BF16),
            pltpu.VMEM((inner, CORES, planes, groups + 1, GROUP, CHUNK), BF16),
            pltpu.VMEM((inner, CORES, planes, groups, GROUP, CHUNK), BF16),
            pltpu.VMEM((2, depth, CHUNK), BF16),
            pltpu.VMEM((planes, local, 2 * rank, depth), BF16),
            pltpu.VMEM((planes, 8, 128), jnp.int32),
            pltpu.SMEM((planes, 8, 128), jnp.int32),
            pltpu.VMEM((planes, groups, GROUP, CHUNK), BF16),
            pltpu.VMEM((planes, groups + STATS, GROUP, CHUNK), BF16),
            pltpu.VMEM((chunks, groups, GROUP, CHUNK), BF16),
            pltpu.VMEM((chunks, groups + STATS, GROUP, CHUNK), BF16),
            dma((5,)),
            dma((chunks,)),
            dma((chunks, 2)),
            dma,
            dma((2,)),
            dma((chunks, 2)),
            dma((chunks, 2)),
            dma((chunks, 2, 2)),
            dma((chunks, 2, 2)),
            dma((planes,)),
            dma((planes,)),
            dma((planes,)),
            dma((planes,)),
            dma((2, chunks)),
            dma((2, planes)),
            dma((2, inner)),
            dma((2, inner)),
            dma((2, inner)),
            dma((2, inner)),
            dma((2, planes)),
            dma((2, chunks)),
        ],
        compiler_params=pltpu.CompilerParams(
            collective_id=0, has_side_effects=True, vmem_limit_bytes=28 * 1024 * 1024 + moved
        ),
    )(
        *(
            pltpu.with_memory_space_constraint(x, pltpu.HBM)
            for x in (
                near_cols,
                near_count,
                far_cols,
                sources,
                self_terms,
                near_tiles,
                jnp.swapaxes(basis_left, 1, 2),
                jnp.swapaxes(basis_right, 1, 2),
                couplings,
            )
        )
    )
    return pl.pallas_call(
        hand_over,
        out_shape=tuple(jax.ShapeDtypeStruct(r.shape, r.dtype) for r in results),
        in_specs=(anywhere,) * 3,
        out_specs=(anywhere,) * 3,
        scratch_shapes=[dma((3,))],
        compiler_params=pltpu.CompilerParams(vmem_limit_bytes=1024 * 1024),
    )(*results)


def solution(mesh):
    placed = (
        P(("groups", "store"), None),
        P(None, "store"),
        P(None, "store", None, None, None),
        P("store", None),
        P("store"),
        P("store", None),
        P("store", None, None),
        P("store", None, None),
        P(None, "store", None, None, None),
    )
    return jax.shard_map(
        functools.partial(shards, mesh.shape["store"]),
        mesh=mesh,
        in_specs=placed,
        out_specs=(P(None, ("groups", "store"), None), P("groups", None), P("groups", None)),
        check_vma=False,
    )
```

```python
import functools

import jax
import jax.numpy as jnp
from jax import lax
from jax.experimental import pallas as pl
from jax.experimental.pallas import tpu as pltpu
from jax.sharding import PartitionSpec as P

REACH = 2
EPSILON = 1e-06
CHUNK = 128
GROUP = 16
STATS = 3
PACE = (2, 1, 0, 0, 2, 2, 0)
CORES = 2
TINY = 1e-30
MESH = pl.DeviceIdType.MESH
F32 = jnp.float32
BF16 = jnp.bfloat16


def grid_of(devices):
    chips = devices // CORES
    inner = 1
    while inner * inner * 4 <= chips:
        inner *= 2
    return chips // inner, inner


def chunks_of(columns):
    return columns // CHUNK


def split3(x):
    high = x.astype(BF16)
    rest = x - high.astype(F32)
    mid = rest.astype(BF16)
    low = (rest - mid.astype(F32)).astype(BF16)
    return [high.astype(F32), mid.astype(F32), low.astype(F32)]


def kernel(
    devices,
    cols_ref,
    count_ref,
    far_ref,
    src_hbm,
    self_hbm,
    tiles_hbm,
    left_hbm,
    right_hbm,
    coup_hbm,
    out_any,
    heights_any,
    norms_any,
    self_ref,
    tiles_ref,
    left_ref,
    right_ref,
    coup_ref,
    out_ref,
    heights_ref,
    norms_ref,
    w_ref,
    left_t,
    self_col,
    u1,
    u2,
    uw,
    y_ref,
    zo1,
    zo2,
    zi1,
    zi2,
    zc,
    zsel,
    cm,
    fv,
    fs,
    co1,
    co2,
    ci1,
    ci2,
    in_sem,
    src_sem,
    out_sem,
    fs_sem,
    own_sem,
    h1_send,
    h1_recv,
    h2_send,
    h2_recv,
    m_send,
    m_recv,
    n_send,
    n_recv,
    z_send,
    z_recv,
    y_send,
    y_recv,
    f_send,
    f_recv,
    c_send,
    c_recv,
):
    me = lax.axis_index("store")
    planes, inner = grid_of(devices)
    chips = devices // CORES
    chip = me // CORES
    core = me % CORES
    plane = chip // inner
    place = chip % inner
    homes = planes // chunks_of(src_hbm.shape[1])
    partner = chip * CORES + (1 - core)
    right = (me + 1) % devices
    left = (me + devices - 1) % devices
    local, near, size = tiles_ref.shape[1:4]
    far, rank = coup_ref.shape[2:4]
    rows = local * size
    width = u1.shape[2]
    chunks = u1.shape[0]
    blocks = devices * local
    panels = blocks * size
    pieces = rank // GROUP

    def device_at(a, b, k):
        return (a * inner + b) * CORES + k

    def remote(src, dst, send, recv, peer):
        return pltpu.make_async_remote_copy(
            src_ref=src,
            dst_ref=dst,
            send_sem=send,
            recv_sem=recv,
            device_id={"store": peer},
            device_id_type=MESH,
        )

    barrier = pltpu.get_barrier_semaphore()

    def greet(peer):
        pl.semaphore_signal(barrier, inc=1, device_id={"store": peer}, device_id_type=MESH)

    greet(left)
    greet(right)
    for t in range(1, inner):
        to = (place + t) % inner
        greet(device_at(plane, to, core))
    for t in range(1, planes):
        greet(device_at((plane + t) % planes, place, core))

    def own_copy(c):
        return pltpu.make_async_copy(
            src_hbm.at[:, pl.ds(c * width, width)],
            u1.at[c, pl.ds(rows, rows)],
            src_sem.at[c],
        )

    loads = [
        pltpu.make_async_copy(hbm, vmem, in_sem.at[i])
        for i, (hbm, vmem) in enumerate(
            (
                (right_hbm, right_ref),
                (tiles_hbm, tiles_ref),
                (left_hbm, left_ref),
                (coup_hbm, coup_ref),
                (self_hbm, self_ref),
            )
        )
    ]
    loads[0].start()
    for c in range(chunks):
        own_copy(c).start()
    for load in loads[1:]:
        load.start()

    def halo1(c):
        own = src_hbm.at[:, pl.ds(c * width, width)]
        return (
            remote(own, u1.at[c, pl.ds(0, rows)], h1_send.at[c, 0], h1_recv.at[c, 0], right),
            remote(own, u1.at[c, pl.ds(2 * rows, rows)], h1_send.at[c, 1], h1_recv.at[c, 1], left),
        )

    def halo2(c, o):
        field = u2.at[c, o]
        own = field.at[pl.ds(rows, rows)]
        return (
            remote(own, field.at[pl.ds(0, rows)], h2_send.at[c, o, 0], h2_recv.at[c, o, 0], right),
            remote(
                own, field.at[pl.ds(2 * rows, rows)], h2_send.at[c, o, 1], h2_recv.at[c, o, 1], left
            ),
        )

    def home(c):
        return c * homes

    has_home = plane % homes == 0
    mine = plane // homes
    groups = local * 2 * pieces

    class Stage:
        def __init__(self, n, zo, zi, co, ci):
            self.n, self.zo, self.zi, self.co, self.ci = n, zo, zi, co, ci

        def give_copy(self, c):
            return remote(
                self.zo.at[c],
                self.zi.at[place, core, plane],
                z_send.at[self.n, c],
                z_recv.at[self.n, plane],
                device_at(home(c), place, core),
            )

        def give(self, c):
            @pl.when(plane == home(c))
            def _():
                self.zi[place, core, plane] = self.zo[c]

            @pl.when(plane != home(c))
            def _():
                self.give_copy(c).start()

        def got(self, source):
            part = self.zi.at[place, core, source]
            return remote(part, part, z_send.at[self.n, 0], z_recv.at[self.n, source], partner)

        def across(self, t, a):
            part = self.zi.at[place, core, a]
            return remote(
                part,
                part,
                y_send.at[self.n, t, a],
                y_recv.at[self.n, place, a],
                device_at(plane, (place + t) % inner, core),
            )

        def crossed(self, source, a):
            part = self.zi.at[source, core, a]
            return remote(
                part, part, y_send.at[self.n, 0, a], y_recv.at[self.n, source, a], partner
            )

        def forward(self, source):
            part = self.zi.at[source, core]
            return remote(part, part, f_send.at[self.n, source], f_recv.at[self.n, source], partner)

        def spread(self):
            @pl.when(has_home)
            def _():
                for i in range(planes):
                    a = (plane + i) % planes
                    if i:
                        self.got(a).wait_recv()
                    for t in range(1, inner):
                        self.across(t, a).start()
                self.forward(place).start()

        def share(self):
            @pl.when(has_home)
            def _():
                for t in range(1, inner):
                    source = (place + t) % inner
                    for a in range(planes):
                        self.crossed(source, a).wait_recv()
                    self.forward(source).start()

        def complete(self):
            @pl.when(has_home)
            def _():
                for b in range(inner):
                    part = self.zi.at[b, 1 - core]
                    remote(
                        part, part, f_send.at[self.n, b], f_recv.at[self.n, b], partner
                    ).wait_recv()

        def back_copy(self, p):
            return remote(
                self.co.at[p],
                self.ci.at[mine],
                c_send.at[self.n, p],
                c_recv.at[self.n, mine],
                device_at(p, place, core),
            )

        def give_back(self):
            @pl.when(has_home)
            def _():
                own = pltpu.make_async_copy(
                    self.co.at[plane], self.ci.at[mine], own_sem.at[self.n]
                )
                own.start()
                for t in range(1, planes):
                    self.back_copy((plane + t) % planes).start()
                own.wait()

        def back(self, c):
            @pl.when(plane != home(c))
            def _():
                part = self.ci.at[c]
                remote(
                    part, part, c_send.at[self.n, 0], c_recv.at[self.n, c], partner
                ).wait_recv()

        def drain(self):
            for c in range(chunks):
                pl.when(plane != home(c))(lambda c=c: self.give_copy(c).wait_send())

            @pl.when(has_home)
            def _():
                for t in range(1, inner):
                    for a in range(planes):
                        self.across(t, a).wait_send()
                for b in range(inner):
                    self.forward(b).wait_send()
                for t in range(1, planes):
                    self.back_copy((plane + t) % planes).wait_send()

    stage1 = Stage(0, zo1, zi1, co1, ci1)
    stage2 = Stage(1, zo2, zi2, co2, ci2)

    def to_coeffs(r, values):
        return (
            jnp.dot(right_ref[r], values, preferred_element_type=F32)
            .astype(BF16)
            .reshape(pieces, GROUP, width)
        )

    def table_copies(t):
        to = device_at((plane + t) % planes, place, core)
        m, n = cm.at[plane], fv.at[plane]
        return (
            remote(n, n, n_send.at[t], n_recv.at[plane], to),
            remote(m, m, m_send.at[t], m_recv.at[plane], to),
        )

    def table_waits(t):
        source = (plane + t) % planes
        m, n = cm.at[source], fv.at[source]
        return (
            remote(n, n, n_send.at[t], n_recv.at[source], partner),
            remote(m, m, m_send.at[t], m_recv.at[source], partner),
        )

    def start1(c):
        if c < chunks:
            for copy in halo1(c):
                copy.start()

    loads[0].wait()
    for c in range(chunks):
        own_copy(c).wait()
        for r in range(local):
            value = to_coeffs(r, u1[c, pl.ds(rows + r * size, size)])
            zo1[c, pl.ds(r * pieces, pieces)] = value
    pl.semaphore_wait(barrier, 2 + inner - 1 + planes - 1)

    for c in range(chunks):
        stage1.give(c)
    start1(0)
    for load in loads[1:]:
        load.wait()
    line = lax.broadcasted_iota(jnp.int32, (8, 128), 0)
    lane = lax.broadcasted_iota(jnp.int32, (8, 128), 1)
    table = jnp.zeros((8, 128), jnp.int32)
    for r in range(local):
        for k in range(far):
            table = jnp.where((line == r) & (lane == k), far_ref[r, k], table)
        for o in range(2):
            parts = [coup_ref[o, r, k] for k in range(far)]
            if cm.shape[3] > far * rank:
                parts.append(jnp.zeros((rank, cm.shape[3] - far * rank), BF16))
            cm[plane, r, pl.ds(o * rank, rank)] = jnp.concatenate(parts, axis=1)
    fv[plane] = table

    for t in range(1, planes):
        for copy in table_copies(t):
            copy.start()

    def prepare(r):
        row = me * local + r
        for d in range(near):
            target = (row + d - REACH + blocks) % blocks
            slot = jnp.int32(0)
            for k in range(1, near):
                slot = jnp.where(cols_ref[r, k] == target, k, slot)
            live = (slot < count_ref[r]).astype(F32).astype(BF16)
            for o in range(2):
                w_ref[r, pl.ds(o * size, size), pl.ds(d * size, size)] = (
                    tiles_ref[o, r, slot] * live
                )
        left_t[r] = left_ref[r].astype(F32).T.astype(BF16)
        diag = lax.broadcasted_iota(jnp.int32, (size, size), 0) == lax.broadcasted_iota(
            jnp.int32, (size, size), 1
        )
        for o in range(2):
            line = self_ref[pl.ds(o, 1), pl.ds(r * size, size)]
            self_col[o, pl.ds(r * size, size)] = jnp.sum(
                jnp.where(diag, line, 0.0), axis=1, keepdims=True
            )

    zsel[...] = jnp.zeros_like(zsel)
    prepare(0)

    def where_is(device):
        return device // CORES % inner, device % CORES, device // CORES // inner

    def chosen(z, p, r, k, scale, o):
        block = fs[p, r, k]
        at = (block % local * scale + o) * pieces
        return z[(*where_is(block // local), pl.ds(at, pieces))].reshape(rank, width)

    def sums1():
        @pl.when(has_home)
        def _():
            for p in range(planes):
                for r in range(local):
                    for k in range(far):
                        zsel[0, pl.ds(k * rank, rank)] = chosen(zi1, p, r, k, 1, 0)
                    value = jnp.dot(cm[p, r], zsel[0], preferred_element_type=F32)
                    co1[p, pl.ds(r * 2 * pieces, 2 * pieces)] = value.astype(BF16).reshape(
                        2 * pieces, GROUP, width
                    )

    def stat(tile, i):
        part = tile[..., 3 * i : 3 * i + 1, :]
        return (
            part
            + tile[..., 3 * i + 1 : 3 * i + 2, :]
            + tile[..., 3 * i + 2 : 3 * i + 3, :]
        )

    def sums2():
        @pl.when(has_home)
        def _():
            every = zi2[:, :, :, groups].astype(F32).reshape(devices, GROUP, width)
            q = stat(every, 0)
            scale = jnp.sum(q, axis=0) / panels
            inv = 1.0 / jnp.sqrt(scale + EPSILON)
            totals = []
            for o in range(2):
                local_h = stat(every, 1 + o)
                h = jnp.sum(local_h * q, axis=0) * inv * inv / panels
                off = local_h - h[None]
                spread = jnp.sum(stat(every, 3 + o) + off * off * q, axis=0) * inv * inv / panels
                norm = jnp.sqrt(spread + EPSILON)
                totals.append((inv / norm, h, norm))
                delta = off.reshape(inner, CORES, planes, 1, 1, width)
                for r in range(local):
                    at = pl.ds((r * 2 + o) * pieces, pieces)
                    base = zi1[:, :, :, pl.ds(r * pieces, pieces)].astype(F32)
                    zc[:, :, :, at] = (zi2[:, :, :, at].astype(F32) + delta * base).astype(BF16)
            for p in range(planes):
                for r in range(local):
                    for o in range(2):
                        for k in range(far):
                            zsel[o, pl.ds(k * rank, rank)] = chosen(zc, p, r, k, 2, o)
                        value = jnp.dot(
                            cm[p, r, pl.ds(o * rank, rank)],
                            zsel[o],
                            preferred_element_type=F32,
                        )
                        co2[p, pl.ds((r * 2 + o) * pieces, pieces)] = value.astype(BF16).reshape(
                            pieces, GROUP, width
                        )
                target = device_at(p, place, core)
                lines = []
                for o in range(2):
                    for shift in (devices - 1, 0, 1):
                        tile = zi2[(*where_is((target + shift) % devices), groups)].astype(F32)
                        lines += split3(stat(tile, 1 + o) - totals[o][1])
                    for x in totals[o]:
                        lines += split3(x)
                lines.append(jnp.zeros((STATS * GROUP - len(lines), width), F32))
                co2[p, pl.ds(groups, STATS)] = (
                    jnp.concatenate(lines, axis=0).astype(BF16).reshape(STATS, GROUP, width)
                )

    def first(c):
        for copy in halo1(c):
            copy.wait_recv()
        for r in range(local):
            total = jnp.dot(
                w_ref[r],
                u1[c, pl.ds(r * size, near * size)],
                preferred_element_type=F32,
            )
            for o in range(2):
                y_ref[c, o, pl.ds(r * size, size)] = total[o * size : (o + 1) * size]

    def second(c):
        stage1.back(c)
        q = jnp.zeros((1, width), F32)
        p = [jnp.zeros((1, width), F32) for _ in range(2)]
        for r in range(local):
            own = u1[c, pl.ds(rows + r * size, size)].astype(F32)
            q += jnp.sum(own * own, axis=0, keepdims=True)
            for o in range(2):
                at = pl.ds(r * size, size)
                coeffs = ci1[c, pl.ds((r * 2 + o) * pieces, pieces)].reshape(rank, width)
                more = jnp.dot(left_t[r], coeffs, preferred_element_type=F32)
                value = y_ref[c, o, at] + more + self_col[o, at] * own
                y_ref[c, o, at] = value
                p[o] += jnp.sum(value * own, axis=0, keepdims=True)
        h = [p[o] / jnp.maximum(q, TINY) for o in range(2)]
        rest = []
        own = u1[c, pl.ds(rows, rows)].astype(F32)
        for o in range(2):
            rem = y_ref[c, o] - h[o] * own
            rest.append(jnp.sum(rem * rem, axis=0, keepdims=True))
            value = rem.astype(BF16)
            u2[c, o, pl.ds(rows, rows)] = value
            for r in range(local):
                zo2[c, pl.ds((r * 2 + o) * pieces, pieces)] = to_coeffs(
                    r, value[r * size : (r + 1) * size]
                )
        lines = []
        for x in (q, *h, *rest):
            lines += split3(x)
        lines.append(jnp.zeros((GROUP - len(lines), width), F32))
        zo2[c, groups] = jnp.concatenate(lines, axis=0).astype(BF16)
        stage2.give(c)

    def third(c):
        cut = pl.ds(c * width, width)
        stage2.back(c)
        told = ci2[c, pl.ds(groups, STATS)].astype(F32).reshape(STATS * GROUP, width)
        for o in range(2):
            factor, h, norm = (stat(told, 6 * o + i) for i in range(3, 6))
            heights_ref[pl.ds(o, 1), cut] = h
            norms_ref[pl.ds(o, 1), cut] = norm
            for copy in halo2(c, o):
                copy.wait_recv()
            for i in range(3):
                at = pl.ds(i * rows, rows)
                delta = stat(told, 6 * o + i)
                uw[at] = (u2[c, o, at].astype(F32) + delta * u1[c, at].astype(F32)).astype(BF16)
            for r in range(local):
                at = pl.ds(r * size, size)
                coeffs = ci2[c, pl.ds((r * 2 + o) * pieces, pieces)].reshape(rank, width)
                total = jnp.dot(
                    w_ref[r, pl.ds(o * size, size)],
                    uw[pl.ds(r * size, near * size)],
                    preferred_element_type=F32,
                )
                total += jnp.dot(left_t[r], coeffs, preferred_element_type=F32)
                own = uw[pl.ds(rows + r * size, size)].astype(F32)
                out_ref[o, at, cut] = (total + self_col[o, at] * own) * factor
            copy_out(c, o).start()

    def copy_out(c, o):
        cut = pl.ds(c * width, width)
        return pltpu.make_async_copy(out_ref.at[o, :, cut], out_any.at[o, :, cut], out_sem.at[c, o])

    sent = []

    def send(count):
        for _ in range(count):
            n = len(sent)
            if n < 2 * chunks:
                sent.append(n)
                for copy in halo2(n // 2, n % 2):
                    copy.start()

    stage1.spread()
    start1(1)
    for r in range(1, local):
        prepare(r)
    stage1.share()
    start1(2)
    for t in range(1, planes):
        for copy in table_waits(t):
            copy.wait_recv()
    index = pltpu.make_async_copy(fv, fs, fs_sem)
    index.start()
    first(0)
    stage1.complete()
    index.wait()
    sums1()
    stage1.give_back()
    for c in range(3, chunks):
        start1(c)
    done = (0, 1)
    first(1)
    for c in range(chunks):
        second(c)
        send(PACE[min(c, 3)])
        if c + 1 < chunks and c + 1 not in done:
            first(c + 1)
    stage2.spread()
    send(PACE[4])
    stage2.share()
    send(PACE[5])
    stage2.complete()
    send(PACE[6])
    sums2()
    stage2.give_back()
    send(2 * chunks)
    for c in range(chunks):
        third(c)

    small = (
        pltpu.make_async_copy(heights_ref, heights_any, in_sem.at[0]),
        pltpu.make_async_copy(norms_ref, norms_any, in_sem.at[1]),
    )
    for copy in small:
        copy.start()
    for c in range(chunks):
        for copy in halo1(c):
            copy.wait_send()
        for o in range(2):
            for copy in halo2(c, o):
                copy.wait_send()
    stage1.drain()
    stage2.drain()
    for t in range(1, planes):
        for copy in table_copies(t):
            copy.wait_send()
    for copy in small:
        copy.wait()
    for c in range(chunks):
        for o in range(2):
            copy_out(c, o).wait()


def hand_over(images_ref, heights_ref, norms_ref, out_images, out_heights, out_norms, sem):
    copies = [
        pltpu.make_async_copy(a, b, sem.at[i])
        for i, (a, b) in enumerate(
            (
                (images_ref, out_images),
                (heights_ref, out_heights),
                (norms_ref, out_norms),
            )
        )
    ]
    for copy in copies:
        copy.start()
    for copy in copies:
        copy.wait()


def shards(
    devices,
    sources,
    self_terms,
    near_tiles,
    near_cols,
    near_count,
    far_cols,
    basis_left,
    basis_right,
    couplings,
):
    rows, columns = sources.shape
    local, near, size = near_tiles.shape[1:4]
    far, rank = couplings.shape[2:4]
    chunks = columns // CHUNK
    planes, inner = grid_of(devices)
    depth = -(-far * rank // 128) * 128
    pieces = rank // GROUP
    dma = pltpu.SemaphoreType.DMA
    smem = pl.BlockSpec(memory_space=pltpu.SMEM)
    hbm = pl.BlockSpec(memory_space=pltpu.HBM)
    anywhere = pl.BlockSpec(memory_space=pl.ANY)
    moved = devices * (5 * local * rank + GROUP) * CHUNK * 2
    groups = 2 * local * pieces
    results = pl.pallas_call(
        functools.partial(kernel, devices),
        out_shape=(
            jax.ShapeDtypeStruct((2, rows, columns), F32),
            jax.ShapeDtypeStruct((2, columns), F32),
            jax.ShapeDtypeStruct((2, columns), F32),
        ),
        in_specs=[smem] * 3 + [hbm] * 6,
        out_specs=(anywhere,) * 3,
        scratch_shapes=[
            pltpu.VMEM(self_terms.shape, F32),
            pltpu.VMEM(near_tiles.shape, BF16),
            pltpu.VMEM((local, rank, size), BF16),
            pltpu.VMEM((local, rank, size), BF16),
            pltpu.VMEM(couplings.shape, BF16),
            pltpu.VMEM((2, rows, columns), F32),
            pltpu.VMEM((2, columns), F32),
            pltpu.VMEM((2, columns), F32),
            pltpu.VMEM((local, 2 * size, near * size), BF16),
            pltpu.VMEM((local, size, rank), BF16),
            pltpu.VMEM((2, rows, 1), F32),
            pltpu.VMEM((chunks, 3 * rows, CHUNK), BF16),
            pltpu.VMEM((chunks, 2, 3 * rows, CHUNK), BF16),
            pltpu.VMEM((3 * rows, CHUNK), BF16),
            pltpu.VMEM((chunks, 2, rows, CHUNK), F32),
            pltpu.VMEM((chunks, groups // 2, GROUP, CHUNK), BF16),
            pltpu.VMEM((chunks, groups + 1, GROUP, CHUNK), BF16),
            pltpu.VMEM((inner, CORES, planes, groups // 2, GROUP, CHUNK), BF16),
            pltpu.VMEM((inner, CORES, planes, groups + 1, GROUP, CHUNK), BF16),
            pltpu.VMEM((inner, CORES, planes, groups, GROUP, CHUNK), BF16),
            pltpu.VMEM((2, depth, CHUNK), BF16),
            pltpu.VMEM((planes, local, 2 * rank, depth), BF16),
            pltpu.VMEM((planes, 8, 128), jnp.int32),
            pltpu.SMEM((planes, 8, 128), jnp.int32),
            pltpu.VMEM((planes, groups, GROUP, CHUNK), BF16),
            pltpu.VMEM((planes, groups + STATS, GROUP, CHUNK), BF16),
            pltpu.VMEM((chunks, groups, GROUP, CHUNK), BF16),
            pltpu.VMEM((chunks, groups + STATS, GROUP, CHUNK), BF16),
            dma((5,)),
            dma((chunks,)),
            dma((chunks, 2)),
            dma,
            dma((2,)),
            dma((chunks, 2)),
            dma((chunks, 2)),
            dma((chunks, 2, 2)),
            dma((chunks, 2, 2)),
            dma((planes,)),
            dma((planes,)),
            dma((planes,)),
            dma((planes,)),
            dma((2, chunks)),
            dma((2, planes)),
            dma((2, inner, planes)),
            dma((2, inner, planes)),
            dma((2, inner)),
            dma((2, inner)),
            dma((2, planes)),
            dma((2, chunks)),
        ],
        compiler_params=pltpu.CompilerParams(
            collective_id=0, has_side_effects=True, vmem_limit_bytes=28 * 1024 * 1024 + moved
        ),
    )(
        *(
            pltpu.with_memory_space_constraint(x, pltpu.HBM)
            for x in (
                near_cols,
                near_count,
                far_cols,
                sources,
                self_terms,
                near_tiles,
                jnp.swapaxes(basis_left, 1, 2),
                jnp.swapaxes(basis_right, 1, 2),
                couplings,
            )
        )
    )
    return pl.pallas_call(
        hand_over,
        out_shape=tuple(jax.ShapeDtypeStruct(r.shape, r.dtype) for r in results),
        in_specs=(anywhere,) * 3,
        out_specs=(anywhere,) * 3,
        scratch_shapes=[dma((3,))],
        compiler_params=pltpu.CompilerParams(vmem_limit_bytes=1024 * 1024),
    )(*results)


def solution(mesh):
    placed = (
        P(("groups", "store"), None),
        P(None, "store"),
        P(None, "store", None, None, None),
        P("store", None),
        P("store"),
        P("store", None),
        P("store", None, None),
        P("store", None, None),
        P(None, "store", None, None, None),
    )
    return jax.shard_map(
        functools.partial(shards, mesh.shape["store"]),
        mesh=mesh,
        in_specs=placed,
        out_specs=(P(None, ("groups", "store"), None), P("groups", None), P("groups", None)),
        check_vma=False,
    )
```
